128 devices in a mesh: row: 8 (over z, x_hi), blk: 16 (over y, x_lo, core).
Axes of the slice: x: 4 (x_hi: 2, x_lo: 2; x = x_hi * 2 + x_lo), y: 4, z: 4, core: 2. Of those that a mesh axis runs over, the one named last changes fastest.
Arguments:
- amplitudes: bfloat16 [8192, 131072], P('blk', 'row'), may hold values from -6 to 6
- integrals: bfloat16 [131072, 512], P('row', 'blk'), may hold values from -0.0234375 to 0.0234375
- live_pairs: int32 [32], P('row'), may hold values from 0 to 1, as said below
- slab_amplitudes: bfloat16 [64, 128, 512], P('row', 'blk'), may hold values from -6 to 6
- cycle_integrals: bfloat16 [2048, 2048], P('row', 'blk'), may hold values from -0.125 to 0.125
Outputs:
- residual: bfloat16 [8192, 512], P('blk', 'row')
The draws below stay inside these ranges and needn't reach their ends.
Inputs may be any that keep to these rules, and one draw needn't show every extreme that they name: `live_pairs`: within each aligned group of 4 slots (slots g * 4 to g * 4 + 3) exactly 2 slots are live.
All inputs are finite; a program needn't handle non-finite values.
Results may differ from the reference program's by a relative error of at most 0.001.
Values may be sent and summed in bfloat16 or wider, within the bound.
No kernel may reach another device: no remote copies, remote signals or barrier semaphores. Data moves between devices by JAX's collectives and lax.ppermute only.
A program may use at most 192 MiB of HBM per device.

```python
import jax
import jax.numpy as jnp

OI = 128
OW = 64
TS = 64
KP_DEV = 4
SA = 16
SB = 32
KP = 32


def draw_live_pairs(key, part):
    key = jax.random.fold_in(key, 7)
    groups = KP // KP_DEV
    scores = jax.random.randint(key, (groups, KP_DEV), 0, 1 << 20) * KP_DEV + jnp.arange(KP_DEV)[None, :]
    rank_order = jnp.argsort(jnp.argsort(scores, axis=1), axis=1)
    return (rank_order < KP_DEV // 2).astype(jnp.int32).reshape(KP)


def strengthened(entries, key, source, target, blocks, factor):
    def block_of(axis_at):
        return (jnp.arange(entries.shape[axis_at]) // (entries.shape[axis_at] // blocks)).reshape((-1,) + (1,) * (entries.ndim - 1 - axis_at))

    first = jax.random.permutation(key, blocks)[block_of(target)]
    far = (block_of(target) + blocks // 2) % blocks
    return jnp.where((block_of(source) == first) | (block_of(source) == far), factor * entries, entries)


def block_levels(stream_key, extent, shards, smallest, high):
    level, own = 1.0, jax.random.fold_in(stream_key, 6)
    for axis_at, shards_of in shards:
        steps = jnp.exp(jax.random.uniform(jax.random.fold_in(own, axis_at), (shards_of,), jnp.float32, smallest / len(shards), high / len(shards)))
        level = level * jnp.repeat(steps, extent[axis_at] // shards_of).reshape([-1 if axis == axis_at else 1 for axis in range(len(extent))])
    return level


def normal_values(key, extent, width, most, cuts=(), kind=jnp.bfloat16):
    factor_of = block_levels(key, extent, cuts, -0.22, 0.18) if cuts else 1.0
    entries = jax.random.normal(key, extent, jnp.float32) * width * factor_of
    return jnp.minimum(jnp.maximum(entries, -most), most).astype(kind)


def gaussian_with(rng, shape, scale, reach, pieces, heavy, held_as=jnp.bfloat16):
    values = scale * jax.random.normal(rng, shape, jnp.float32)
    if pieces:
        values = values * block_levels(rng, shape, pieces, -0.22, 0.18)
    return jnp.clip(strengthened(values, jax.random.fold_in(rng, 3), *heavy), -reach, reach).astype(held_as)


def setup_inputs(seed: int = 0) -> dict:
    streams_of = jax.random.split(jax.random.key(seed), 6)
    amplitudes = normal_values(streams_of[0], (OI * OW, KP * TS * TS), 1.0, 6.0, ((0, 16), (1, 8)))
    integrals = gaussian_with(streams_of[1], (KP * TS * TS, SA * SB), (KP * TS * TS) ** -0.5, 0.0234375, ((0, 8), (1, 16)), (0, 1, 16, 2.0))
    live_pairs = draw_live_pairs(jax.random.fold_in(streams_of[5], 71), 0)
    slab_amplitudes = normal_values(streams_of[3], (OW, OI, SA * SB), 1.0, 6.0, ((0, 8), (1, 16)))
    cycle_integrals = normal_values(streams_of[4], (OW * SB, OW * SB), (OW * SB) ** -0.5, 0.125, ((0, 8), (1, 16)))
    return {"amplitudes": amplitudes, "integrals": integrals, "live_pairs": live_pairs, "slab_amplitudes": slab_amplitudes, "cycle_integrals": cycle_integrals}


def reference(amplitudes, integrals, live_pairs, slab_amplitudes, cycle_integrals):
    tile_size = TS * TS
    weights = jnp.repeat(live_pairs, tile_size, total_repeat_length=KP * tile_size).astype(jnp.bfloat16)
    masked = integrals * weights[:, None]
    ladder = jnp.dot(amplitudes, masked, preferred_element_type=jnp.float32)
    slab_amps = slab_amplitudes.astype(jnp.float32).reshape(OW, OI, SA, SB)
    cycle_blocks = cycle_integrals.astype(jnp.float32).reshape(OW, SB, OW, SB)
    cycle_term = jnp.einsum("kiac,kcjb->ijab", slab_amps, cycle_blocks).reshape(OI * OW, SA * SB)
    return (ladder + cycle_term).astype(jnp.bfloat16)
```

```python
import jax
import jax.numpy as jnp
from jax import lax
from jax.sharding import PartitionSpec as P

OW = 64
TS = 64
SB = 32
LIVE = 2


def per_device(amplitudes, integrals, live_pairs, slab_amplitudes, cycle_integrals):
    tile = TS * TS
    slots = live_pairs.shape[0]
    order = jnp.argsort(1 - live_pairs, stable=True)[:LIVE]
    columns = integrals.T.reshape(-1, slots, tile)
    live_columns = jnp.concatenate(
        [lax.dynamic_index_in_dim(columns, order[n], 1, keepdims=False) for n in range(LIVE)], axis=1
    )
    live_amps = jnp.concatenate(
        [lax.dynamic_slice_in_dim(amplitudes, order[n] * tile, tile, 1) for n in range(LIVE)], axis=1
    )
    cycle_local = lax.all_gather(cycle_integrals, "blk", axis=1, tiled=True)
    gathered = lax.all_gather(live_columns, "blk", axis=0, tiled=True)

    k_local, i_local, ac = slab_amplitudes.shape
    a_all = ac // SB
    slab = slab_amplitudes.reshape(k_local, i_local, a_all, SB).transpose(2, 1, 0, 3)
    slab = slab.reshape(a_all * i_local, k_local * SB)
    cycle = jnp.dot(slab, cycle_local, preferred_element_type=jnp.float32)
    cycle = cycle.reshape(a_all, i_local, OW, SB).transpose(0, 3, 1, 2).reshape(a_all * SB, i_local * OW)

    partial_sums = lax.dot_general(
        gathered, live_amps, (((1,), (1,)), ((), ())), preferred_element_type=jnp.float32
    )
    partial_sums = partial_sums + cycle
    rows = lax.psum(1, "row")
    parts = lax.all_to_all(partial_sums.reshape(rows, -1, partial_sums.shape[1]), "row", 0, 0)
    return jnp.sum(parts, axis=0).astype(jnp.bfloat16).T


def solution(mesh):
    return jax.shard_map(
        per_device,
        mesh=mesh,
        in_specs=(
            P("blk", "row"),
            P("row", "blk"),
            P("row"),
            P("row", "blk", None),
            P("row", "blk"),
        ),
        out_specs=P("blk", "row"),
        check_vma=False,
    )
```

```python
import functools

import jax
import jax.numpy as jnp
from jax import lax
from jax.experimental import pallas as pl
from jax.experimental.pallas import tpu as pltpu
from jax.sharding import PartitionSpec as P

OW = 64
TS = 64
SB = 32
TILE = TS * TS
NY, NX, NC = 4, 2, 2
NZ, NH = 4, 2
HALF = SB // 2
STEP = 1024
KT = TILE // STEP
MIB = 1 << 20


def blk_moves(dy, dx, dc):
    spots = [(y, x, c) for y in range(NY) for x in range(NX) for c in range(NC)]
    index = lambda y, x, c: ((y % NY) * NX + x % NX) * NC + c % NC
    return [(index(y, x, c), index(y + dy, x + dx, c + dc)) for y, x, c in spots]


def row_moves(dz, dx):
    spots = [(z, x) for z in range(NZ) for x in range(NH)]
    index = lambda z, x: (z % NZ) * NH + x % NH
    return [(index(z, x), index(z + dz, x + dx)) for z, x in spots]


def move(value, dy=0, dx=0, dc=0):
    return lax.ppermute(value, "blk", blk_moves(dy, dx, dc))


def move_row(value, dz=0, dx=0):
    return lax.ppermute(value, "row", row_moves(dz, dx))


def live_slot(live, n):
    if n == 0:
        return jnp.where(live[0] == 1, 0, jnp.where(live[1] == 1, 1, 2))
    return jnp.where(live[3] == 1, 3, jnp.where(live[2] == 1, 2, 1))


def pick_kernel(live, columns, first, second, sems):
    copies = []
    for n in range(2):
        start = pl.multiple_of(live_slot(live, n) * TILE, TILE)
        for h, out in enumerate((first, second)):
            copies.append(
                pltpu.make_async_copy(
                    columns.at[pl.ds(h * HALF, HALF), pl.ds(start, TILE)], out.at[n], sems.at[n, h]
                )
            )
    for copy in copies:
        copy.start()
    for copy in copies:
        copy.wait()


def pick_live(live_pairs, columns):
    shape = jax.ShapeDtypeStruct((2, HALF, TILE), columns.dtype)
    return pl.pallas_call(
        pick_kernel,
        out_shape=(shape, shape),
        in_specs=[pl.BlockSpec(memory_space=pltpu.SMEM), pl.BlockSpec(memory_space=pl.ANY)],
        out_specs=(pl.BlockSpec(memory_space=pltpu.VMEM),) * 2,
        scratch_shapes=[pltpu.SemaphoreType.DMA((2, 2))],
        name="pick_live",
    )(live_pairs, columns)


def load_kernel(live, amps, after, out, sems):
    copies = []
    for n in range(2):
        for k in range(KT):
            start = pl.multiple_of(live_slot(live, n) * TILE + k * STEP, STEP)
            at = n * KT + k
            copies.append(pltpu.make_async_copy(amps.at[:, pl.ds(start, STEP)], out.at[at], sems.at[at]))
    for copy in copies:
        copy.start()
    for copy in copies:
        copy.wait()


def load_live(live_pairs, amplitudes, after):
    rows = amplitudes.shape[0]
    return pl.pallas_call(
        load_kernel,
        out_shape=jax.ShapeDtypeStruct((2 * KT, rows, STEP), amplitudes.dtype),
        in_specs=[pl.BlockSpec(memory_space=pltpu.SMEM)] + [pl.BlockSpec(memory_space=pl.ANY)] * 2,
        out_specs=pl.BlockSpec(memory_space=pltpu.VMEM),
        scratch_shapes=[pltpu.SemaphoreType.DMA((2 * KT,))],
        compiler_params=pltpu.CompilerParams(vmem_limit_bytes=40 * MIB),
        name="load_live",
    )(live_pairs, amplitudes, after)


def ladder_kernel(places, count, half, amps, cycle, *refs):
    pieces, outs, total = refs[:count], refs[count : count + NZ], refs[count + NZ]
    for n in range(2):
        held = {tuple(place): pieces[piece].at[index] for piece, index, slot, *place in places if slot == n}
        for k in range(KT):
            cols = slice(k * STEP, (k + 1) * STEP)
            block = jnp.concatenate(
                [held[dy, e, g][:, cols] for dy in range(NY) for e in range(NX) for g in range(NC)]
            )
            term = lax.dot_general(
                block, amps[n * KT + k], (((1,), (1,)), ((), ())), preferred_element_type=jnp.float32
            )
            if n == k == 0:
                total[...] = term
            else:
                total[...] += term

    spot = lax.axis_index("blk")
    y, x, c = spot // (NX * NC), (spot // NC) % NX, spot % NC
    line = lax.axis_index("row")
    z, xh = line // NH, line % NH
    for dz in range(NZ):
        for f in range(NH):
            for core in range(NC):
                dy, e, g = (z + dz + NY - y) % NY, (xh + f + NX - x) % NX, (core + NC - c) % NC
                here = ((dy * NX + e) * NC + g) * HALF
                there = (((z + dz) % NZ) * NH + (xh + f) % NH) * NC + core
                there = there * SB + half * HALF
                there = pl.ds(pl.multiple_of(there, HALF), HALF)
                outs[dz][f, core * HALF : (core + 1) * HALF, :] = total[
                    pl.ds(pl.multiple_of(here, HALF), HALF), :
                ] + jnp.concatenate([cycle[n, there, :] for n in range(cycle.shape[0])], axis=1)


def ladder(half, amplitudes, cycle, pieces):
    places = [(n, *place) for n, (_, held) in enumerate(pieces) for place in held]
    places = [(n, index, slot, dy % NY, e, g) for n, index, slot, dy, e, g in places]
    arrays = [array for array, _ in pieces]
    rows = amplitudes.shape[1]
    q = NY * NX * NC * HALF
    out = jax.ShapeDtypeStruct((NH, q // (NZ * NH), rows), jnp.float32)
    return pl.pallas_call(
        functools.partial(ladder_kernel, places, len(arrays), half),
        out_shape=(out,) * NZ,
        in_specs=[pl.BlockSpec(memory_space=pltpu.VMEM)] * (2 + len(arrays)),
        out_specs=[pl.BlockSpec(memory_space=pltpu.VMEM)] * NZ,
        scratch_shapes=[pltpu.VMEM((q, rows), jnp.float32)],
        compiler_params=pltpu.CompilerParams(vmem_limit_bytes=24 * MIB),
        cost_estimate=pl.CostEstimate(
            flops=2 * q * rows * 2 * TILE, bytes_accessed=2 * q * 2 * TILE, transcendentals=0
        ),
        name="ladder",
    )(amplitudes, cycle, *arrays)


def gather_cycle(cycle_integrals, ready):
    pair = jnp.stack([cycle_integrals, move(cycle_integrals, dx=1)])
    pair, _ = lax.optimization_barrier((pair, ready))
    four = jnp.stack([pair, move(pair, dy=-1), move(pair, dy=2), move(pair, dy=1)])
    return jnp.stack([four, move(four, dc=1)])


def cycle_kernel(slab, blocks, out, turned):
    spot = lax.axis_index("blk")
    y, x, c = spot // (NX * NC), (spot // NC) % NX, spot % NC
    width = blocks.shape[-1]
    pairs = slab.shape[0]
    for block in range(NY * NX * NC):
        dy = (block // (NX * NC) + NY - y) % NY
        e = (block // NC + NX - x) % NX
        g = (block + NC - c) % NC
        term = jnp.dot(slab[...], blocks[g, dy, e], preferred_element_type=jnp.float32)
        turned[block * width : (block + 1) * width, :] = term.T
    a_all = pairs // (2 * out.shape[0])
    for b in range(SB):
        rows = turned[pl.ds(b, OW, stride=SB), :].T
        for i in range(0, pairs // a_all, 2):
            both = [rows[at * a_all : (at + 1) * a_all] for at in (i, i + 1)]
            out[i // 2, pl.ds(b, a_all, stride=SB), :] = jnp.concatenate(both, axis=1)


def cycle_sums(slab_amplitudes, blocks):
    k_local, i_local, ac = slab_amplitudes.shape
    a_all = ac // SB
    slab = slab_amplitudes.reshape(k_local, i_local, a_all, SB).transpose(1, 2, 0, 3)
    slab = slab.reshape(i_local * a_all, k_local * SB)
    return pl.pallas_call(
        cycle_kernel,
        out_shape=jax.ShapeDtypeStruct((i_local // 2, a_all * SB, 2 * OW), jnp.float32),
        in_specs=[pl.BlockSpec(memory_space=pltpu.VMEM)] * 2,
        out_specs=pl.BlockSpec(memory_space=pltpu.VMEM),
        scratch_shapes=[pltpu.VMEM((OW * SB, i_local * a_all), jnp.float32)],
        compiler_params=pltpu.CompilerParams(vmem_limit_bytes=16 * MIB),
        cost_estimate=pl.CostEstimate(flops=1 << 28, bytes_accessed=1 << 23, transcendentals=0),
        name="cycle",
    )(slab, blocks)


def sum_rows(parts):
    total = parts[0]
    for dz in range(1, NZ):
        total = total + move_row(parts[dz], dz=dz)
    return total[0] + move_row(total[1], dx=1)


def per_device(amplitudes, integrals, live_pairs, slab_amplitudes, cycle_integrals):
    x0, y0 = pick_live(live_pairs, integrals.T)
    y_below, y_above, x1 = move(y0, dy=1), move(y0, dy=-1), move(x0, dx=1)
    y1 = move(y0, dx=1)
    slab_amplitudes, _ = lax.optimization_barrier((slab_amplitudes, x1))
    y_far = jnp.stack([move(y_below[0], dy=1), move(y_above[1], dy=-1)])
    x_pair = jnp.stack([x0, x1])
    x_below, x_above = move(x_pair, dy=1), move(x_pair, dy=-1)
    cycle_blocks = gather_cycle(cycle_integrals, x1)
    y_near = jnp.stack([y_below, y_above])
    y_near_1 = move(y_near, dx=1)
    amplitudes, _ = lax.optimization_barrier((amplitudes, y_far))
    live_amps = load_live(live_pairs, amplitudes, y0)
    x_far = jnp.stack([move(x_below[0], dy=1), move(x_above[1], dy=-1)])
    y_far_1 = move(y_far, dx=1)
    cycle = cycle_sums(slab_amplitudes, cycle_blocks)

    def cores(array, spots):
        return [
            (both, [(index, slot, dy, e, g) for index, slot, dy, e in spots])
            for g, both in enumerate((array, move(array, dc=1)))
        ]

    first = []
    for dy, array in ((0, x_pair), (-1, x_below), (1, x_above), (2, x_far)):
        first += cores(array, [((e, n), n, dy, e) for e in range(2) for n in range(2)])
    first = sum_rows(ladder(0, live_amps, cycle, first))

    second = []
    for e, array in enumerate((y0, y1)):
        second += cores(array, [((n,), n, 0, e) for n in range(2)])
    for e, array in enumerate((y_near, y_near_1)):
        second += cores(array, [((d, n), n, dy, e) for d, dy in enumerate((-1, 1)) for n in range(2)])
    for e, array in enumerate((y_far, y_far_1)):
        second += cores(array, [((n,), n, 2, e) for n in range(2)])
    second = sum_rows(ladder(1, live_amps, cycle, second))

    rows = amplitudes.shape[0]
    out = jnp.stack([first.reshape(NC, HALF, rows), second.reshape(NC, HALF, rows)], axis=1)
    return out.reshape(NC * SB, rows).astype(jnp.bfloat16).T


def solution(mesh):
    return jax.shard_map(
        per_device,
        mesh=mesh,
        in_specs=(
            P("blk", "row"),
            P("row", "blk"),
            P("row"),
            P("row", "blk", None),
            P("row", "blk"),
        ),
        out_specs=P("blk", "row"),
        check_vma=False,
    )
```

```python
import functools

import jax
import jax.numpy as jnp
from jax import lax
from jax.experimental import pallas as pl
from jax.experimental.pallas import tpu as pltpu
from jax.sharding import PartitionSpec as P

OW = 64
TS = 64
SB = 32
TILE = TS * TS
NY, NX, NC = 4, 2, 2
NZ, NH = 4, 2
HALF = SB // 2
STEP = 1024
KT = TILE // STEP
MIB = 1 << 20


def blk_moves(dy, dx, dc):
    spots = [(y, x, c) for y in range(NY) for x in range(NX) for c in range(NC)]
    index = lambda y, x, c: ((y % NY) * NX + x % NX) * NC + c % NC
    return [(index(y, x, c), index(y + dy, x + dx, c + dc)) for y, x, c in spots]


def row_moves(dz, dx):
    spots = [(z, x) for z in range(NZ) for x in range(NH)]
    index = lambda z, x: (z % NZ) * NH + x % NH
    return [(index(z, x), index(z + dz, x + dx)) for z, x in spots]


def move(value, dy=0, dx=0, dc=0):
    return lax.ppermute(value, "blk", blk_moves(dy, dx, dc))


def move_row(value, dz=0, dx=0):
    return lax.ppermute(value, "row", row_moves(dz, dx))


def together(*values):
    return lax.optimization_barrier(values)


def live_slot(live, n):
    if n == 0:
        return jnp.where(live[0] == 1, 0, jnp.where(live[1] == 1, 1, 2))
    return jnp.where(live[3] == 1, 3, jnp.where(live[2] == 1, 2, 1))


def pick_kernel(live, columns, out, sems):
    copies = []
    for n in range(2):
        start = pl.multiple_of(live_slot(live, n) * TILE, TILE)
        for h in range(2):
            source = columns.at[pl.ds(h * HALF, HALF), pl.ds(start, TILE)]
            copies.append(pltpu.make_async_copy(source, out.at[h, n], sems.at[n, h]))
    for copy in copies:
        copy.start()
    for copy in copies:
        copy.wait()


def pick_live(live_pairs, columns):
    return pl.pallas_call(
        pick_kernel,
        out_shape=jax.ShapeDtypeStruct((2, 2, HALF, TILE), columns.dtype),
        in_specs=[pl.BlockSpec(memory_space=pltpu.SMEM), pl.BlockSpec(memory_space=pl.ANY)],
        out_specs=pl.BlockSpec(memory_space=pltpu.VMEM),
        scratch_shapes=[pltpu.SemaphoreType.DMA((2, 2))],
        compiler_params=pltpu.CompilerParams(vmem_limit_bytes=4 * MIB),
        name="pick_live",
    )(live_pairs, columns)


def load_kernel(live, amps, out, token, sems):
    token[...] = jnp.zeros_like(token)
    copies = []
    for n in range(2):
        for k in range(KT):
            start = pl.multiple_of(live_slot(live, n) * TILE + k * STEP, STEP)
            at = n * KT + k
            copies.append(pltpu.make_async_copy(amps.at[:, pl.ds(start, STEP)], out.at[at], sems.at[at]))
    for copy in copies:
        copy.start()
    for copy in copies:
        copy.wait()


def load_live(live_pairs, amplitudes):
    rows = amplitudes.shape[0]
    return pl.pallas_call(
        load_kernel,
        out_shape=(
            jax.ShapeDtypeStruct((2 * KT, rows, STEP), amplitudes.dtype),
            jax.ShapeDtypeStruct((8, 128), jnp.float32),
        ),
        in_specs=[pl.BlockSpec(memory_space=pltpu.SMEM), pl.BlockSpec(memory_space=pl.ANY)],
        out_specs=(pl.BlockSpec(memory_space=pltpu.VMEM),) * 2,
        scratch_shapes=[pltpu.SemaphoreType.DMA((2 * KT,))],
        compiler_params=pltpu.CompilerParams(vmem_limit_bytes=40 * MIB),
        name="load_live",
    )(live_pairs, amplitudes)


def ladder_kernel(places, e, count, amps, cycle, before, *refs):
    pieces, outs, (token, total) = refs[:count], refs[count : count + NZ], refs[count + NZ :]
    token[...] = jnp.zeros_like(token)
    for n in range(2):
        held = {}
        for piece, index, slot, *place in places:
            if slot == n:
                held[tuple(place)] = pieces[piece].at[index] if index else pieces[piece]
        for k in range(KT):
            cols = slice(k * STEP, (k + 1) * STEP)
            block = jnp.concatenate(
                [held[dy, g, h][:, cols] for dy in range(NY) for g in range(NC) for h in range(2)]
            )
            term = lax.dot_general(
                block, amps[n * KT + k], (((1,), (1,)), ((), ())), preferred_element_type=jnp.float32
            )
            if n == k == 0:
                total[...] = term
            else:
                total[...] += term

    spot = lax.axis_index("blk")
    y, x, c = spot // (NX * NC), (spot // NC) % NX, spot % NC
    z = lax.axis_index("row") // NH
    for dz in range(NZ):
        dy = (z + dz + NY - y) % NY
        for core in range(NC):
            here = (dy * NC + (core + NC - c) % NC) * SB
            there = ((((z + dz) % NZ) * NX + (x + e) % NX) * NC + core) * SB
            there = pl.ds(pl.multiple_of(there, SB), SB)
            outs[dz][core * SB : (core + 1) * SB, :] = total[
                pl.ds(pl.multiple_of(here, SB), SB), :
            ] + jnp.concatenate([cycle[n, there, :] for n in range(cycle.shape[0])], axis=1)


def ladder(e, amplitudes, cycle, before, pieces):
    places = [(n, *place) for n, (_, held) in enumerate(pieces) for place in held]
    places = [(n, index, slot, dy % NY, g, h) for n, index, slot, dy, g, h in places]
    rows, q = amplitudes.shape[1], NY * NC * SB
    out = jax.ShapeDtypeStruct((q // NZ, rows), jnp.float32)
    return pl.pallas_call(
        functools.partial(ladder_kernel, places, e, len(pieces)),
        out_shape=(out,) * NZ + (jax.ShapeDtypeStruct((8, 128), jnp.float32),),
        in_specs=[pl.BlockSpec(memory_space=pltpu.VMEM)] * (3 + len(pieces)),
        out_specs=[pl.BlockSpec(memory_space=pltpu.VMEM)] * (NZ + 1),
        scratch_shapes=[pltpu.VMEM((q, rows), jnp.float32)],
        compiler_params=pltpu.CompilerParams(vmem_limit_bytes=24 * MIB),
        cost_estimate=pl.CostEstimate(
            flops=2 * q * rows * 2 * TILE, bytes_accessed=2 * q * 2 * TILE, transcendentals=0
        ),
        name="ladder",
    )(amplitudes, cycle, before, *[array for array, _ in pieces])


def pack_kernel(own, beside, out):
    for e, block in enumerate((own, beside)):
        for n in range(block.shape[0] // HALF):
            at = (e * (block.shape[0] // HALF) + n) * block.shape[1]
            out[:, at : at + block.shape[1]] = block[n * HALF : (n + 1) * HALF, :]


def pack_pair(own, beside):
    return pl.pallas_call(
        pack_kernel,
        out_shape=jax.ShapeDtypeStruct((HALF, TILE), own.dtype),
        in_specs=[pl.BlockSpec(memory_space=pltpu.VMEM)] * 2,
        out_specs=pl.BlockSpec(memory_space=pltpu.VMEM),
        compiler_params=pltpu.CompilerParams(vmem_limit_bytes=4 * MIB),
        name="pack_pair",
    )(own, beside)


def cycle_kernel(places, width, slab, token, *refs):
    blocks, out, turned = refs[:-2], refs[-2], refs[-1]
    spot = lax.axis_index("blk")
    y, x, c = spot // (NX * NC), (spot // NC) % NX, spot % NC
    pairs, depth = slab.shape
    for piece, index, dy, g in places:
        for e in range(NX):
            tiles = []
            for n in range(depth // HALF):
                at = (e * (depth // HALF) + n) * width
                tiles.append(blocks[piece][(*index, slice(None), slice(at, at + width))])
            term = jnp.dot(slab[...], jnp.concatenate(tiles), preferred_element_type=jnp.float32)
            block = ((y + dy) % NY * NX + (x + e) % NX) * NC + (c + g) % NC
            turned[pl.ds(pl.multiple_of(block * width, width), width), :] = term.T
    a_all = pairs // (2 * out.shape[0])
    for b in range(SB):
        rows = turned[pl.ds(b, OW, stride=SB), :].T
        for i in range(0, pairs // a_all, 2):
            both = [rows[at * a_all : (at + 1) * a_all] for at in (i, i + 1)]
            out[i // 2, pl.ds(b, a_all, stride=SB), :] = jnp.concatenate(both, axis=1)


def slab_matrix(slab_amplitudes):
    k_local, i_local, ac = slab_amplitudes.shape
    slab = slab_amplitudes.reshape(k_local, i_local, ac // SB, SB).transpose(1, 2, 0, 3)
    return slab.reshape(i_local * ac // SB, k_local * SB)


def cycle_sums(slab, pieces, token, i_local):
    a_all, depth = slab.shape[0] // i_local, slab.shape[1]
    places = [(n, index, dy % NY, g) for n, (_, index, dy, g) in enumerate(pieces)]
    width = OW * SB // (NY * NX * NC)
    return pl.pallas_call(
        functools.partial(cycle_kernel, places, width),
        out_shape=jax.ShapeDtypeStruct((i_local // 2, a_all * SB, 2 * OW), jnp.float32),
        in_specs=[pl.BlockSpec(memory_space=pltpu.VMEM)] * (2 + len(pieces)),
        out_specs=pl.BlockSpec(memory_space=pltpu.VMEM),
        scratch_shapes=[pltpu.VMEM((OW * SB, i_local * a_all), jnp.float32)],
        compiler_params=pltpu.CompilerParams(vmem_limit_bytes=16 * MIB),
        cost_estimate=pl.CostEstimate(
            flops=2 * slab.shape[0] * depth * OW * SB, bytes_accessed=8 * MIB, transcendentals=0
        ),
        name="cycle",
    )(slab, token, *[array for array, *_ in pieces])


def sum_along_z(parts):
    total = parts[0]
    for dz in range(1, NZ):
        total = total + move_row(parts[dz], dz=dz)
    return total


def per_device(amplitudes, integrals, live_pairs, slab_amplitudes, cycle_integrals):
    swapped = {}

    def swap(array):
        return move(array, dc=1)

    def cores(array, *spots):
        return [
            (both, [(index, slot, dy, g, h) for index, slot, dy, h in spots])
            for g, both in enumerate((array, swapped[id(array)] if id(array) in swapped else swap(array)))
        ]

    own = pick_live(live_pairs, integrals.T)
    below, above, beside = move(own, dy=1), move(own, dy=-1), move(own, dx=1)
    cycle_beside = move(cycle_integrals, dx=1)
    amplitudes, own_swap = together(amplitudes, swap(own))
    swapped[id(own)] = own_swap
    live_amps, token = load_live(live_pairs, amplitudes)
    slab_rows = slab_matrix(slab_amplitudes)
    cycle_beside, token, slab_rows = together(cycle_beside, token, slab_rows)
    pair = pack_pair(cycle_integrals, cycle_beside)

    below, above, beside, token, slab_rows, pair = together(below, above, beside, token, slab_rows, pair)
    from_below = move(jnp.concatenate([below[0], beside[0], pair[None]]), dy=1)
    from_above = move(jnp.concatenate([above[1], beside[0], pair[None]]), dy=-1)
    across = move(jnp.stack([below[1], above[1]]), dx=1)
    pair_far = move(pair, dy=2)

    pair_far, below, above, beside = together(pair_far, below, above, beside)
    shadow = [swap(array) for array in (below, above, beside)]
    from_below, from_above, across, *shadow = together(from_below, from_above, across, *shadow)
    for array, other in zip((below, above, beside), shadow):
        swapped[id(array)] = other
    last_below = move(jnp.stack([from_below[2], across[0, 0]]), dy=1)
    last_above = move(jnp.stack([from_above[3], across[1, 1]]), dy=-1)

    pairs = jnp.stack([pair, pair_far])
    blocks = []
    for g, array in enumerate((pairs, swap(pairs))):
        blocks += [(array, (0,), 0, g), (array, (1,), 2, g)]
    for dy, array in ((-1, from_below), (1, from_above)):
        swapped[id(array)] = swap(array)
        blocks += [(array, (4,), dy, 0), (swapped[id(array)], (4,), dy, 1)]
    cycle = cycle_sums(slab_rows, blocks, token, slab_amplitudes.shape[1])

    halves = [(h, n) for h in range(2) for n in range(2)]
    near = []
    for dy, array in ((0, own), (-1, below), (1, above)):
        near += cores(array, *[((h, n), n, dy, h) for h, n in halves])
    for h, array in enumerate((from_below, from_above)):
        near += cores(array, *[((n,), n, 2, h) for n in range(2)])
    *near, token = ladder(0, live_amps, cycle, token, near)
    near = sum_along_z(near)

    last_below, last_above, token = together(last_below, last_above, token)
    far = cores(beside, *[((h, n), n, 0, h) for h, n in halves])
    for dy, array in ((-1, from_below), (1, from_above)):
        far += cores(array, *[((2 + n,), n, dy, 0) for n in range(2)])
    far += cores(across, *[((d, n), n, dy, 1) for d, dy in enumerate((-1, 1)) for n in range(2)])
    for n, array in enumerate((last_below, last_above)):
        far += cores(array, *[((h,), n, 2, h) for h in range(2)])
    far = sum_along_z(ladder(1, live_amps, cycle, token, far)[:NZ])

    mine = lax.axis_index("row") % NH == (lax.axis_index("blk") // NC) % NX
    total = jnp.where(mine, near, far) + move_row(jnp.where(mine, far, near), dx=1)
    return total.astype(jnp.bfloat16).T


def solution(mesh):
    return jax.shard_map(
        per_device,
        mesh=mesh,
        in_specs=(
            P("blk", "row"),
            P("row", "blk"),
            P("row"),
            P("row", "blk", None),
            P("row", "blk"),
        ),
        out_specs=P("blk", "row"),
        check_vma=False,
    )
```

```python
import functools

import jax
import jax.numpy as jnp
from jax import lax
from jax.experimental import pallas as pl
from jax.experimental.pallas import tpu as pltpu
from jax.sharding import PartitionSpec as P

OW = 64
TS = 64
SB = 32
TILE = TS * TS
NY, NX, NC = 4, 2, 2
NZ, NH = 4, 2
HALF = SB // 2
STEP = 1024
KT = TILE // STEP
MIB = 1 << 20
LANES = 128


def blk_moves(dy, dx, dc):
    spots = [(y, x, c) for y in range(NY) for x in range(NX) for c in range(NC)]
    index = lambda y, x, c: ((y % NY) * NX + x % NX) * NC + c % NC
    return [(index(y, x, c), index(y + dy, x + dx, c + dc)) for y, x, c in spots]


def row_moves(dz, dx):
    spots = [(z, x) for z in range(NZ) for x in range(NH)]
    index = lambda z, x: (z % NZ) * NH + x % NH
    return [(index(z, x), index(z + dz, x + dx)) for z, x in spots]


def move(value, dy=0, dx=0, dc=0):
    return lax.ppermute(value, "blk", blk_moves(dy, dx, dc))


def move_row(value, dz=0, dx=0):
    return lax.ppermute(value, "row", row_moves(dz, dx))


def together(*values):
    return lax.optimization_barrier(values)


def live_slot(live, n):
    if n == 0:
        return jnp.where(live[0] == 1, 0, jnp.where(live[1] == 1, 1, 2))
    return jnp.where(live[3] == 1, 3, jnp.where(live[2] == 1, 2, 1))


def pick_kernel(live, columns, out, sems):
    copies = []
    for n in range(2):
        start = pl.multiple_of(live_slot(live, n) * TILE, TILE)
        for h in range(2):
            source = columns.at[pl.ds(h * HALF, HALF), pl.ds(start, TILE)]
            copies.append(pltpu.make_async_copy(source, out.at[2 * h + n], sems.at[n, h]))
    for copy in copies:
        copy.start()
    for copy in copies:
        copy.wait()


def pick_live(live_pairs, columns):
    return pl.pallas_call(
        pick_kernel,
        out_shape=jax.ShapeDtypeStruct((4, HALF, TILE), columns.dtype),
        in_specs=[pl.BlockSpec(memory_space=pltpu.SMEM), pl.BlockSpec(memory_space=pltpu.HBM)],
        out_specs=pl.BlockSpec(memory_space=pltpu.VMEM),
        scratch_shapes=[pltpu.SemaphoreType.DMA((2, 2))],
        compiler_params=pltpu.CompilerParams(vmem_limit_bytes=4 * MIB),
        name="pick_live",
    )(live_pairs, columns)


def load_kernel(live, amps, after, out, token, sems):
    token[...] = jnp.zeros_like(token)
    copies = []
    for n in range(2):
        for k in range(KT):
            start = pl.multiple_of(live_slot(live, n) * TILE + k * STEP, STEP)
            at = n * KT + k
            copies.append(pltpu.make_async_copy(amps.at[:, pl.ds(start, STEP)], out.at[at], sems.at[at]))
    for copy in copies:
        copy.start()
    for copy in copies:
        copy.wait()


def load_live(live_pairs, amplitudes, after):
    rows = amplitudes.shape[0]
    return pl.pallas_call(
        load_kernel,
        out_shape=(
            jax.ShapeDtypeStruct((2 * KT, rows, STEP), amplitudes.dtype),
            jax.ShapeDtypeStruct((8, 128), jnp.float32),
        ),
        in_specs=[pl.BlockSpec(memory_space=pltpu.SMEM)] + [pl.BlockSpec(memory_space=pl.ANY)] * 2,
        out_specs=(pl.BlockSpec(memory_space=pltpu.VMEM),) * 2,
        scratch_shapes=[pltpu.SemaphoreType.DMA((2 * KT,))],
        compiler_params=pltpu.CompilerParams(vmem_limit_bytes=40 * MIB),
        name="load_live",
    )(live_pairs, amplitudes, after)


def ladder_kernel(places, e, count, amps, cycle, before, *refs):
    pieces, outs, (token, total) = refs[:count], refs[count : count + NZ], refs[count + NZ :]
    token[...] = jnp.zeros_like(token)
    for n in range(2):
        held = {}
        for piece, index, slot, *place in places:
            if slot == n:
                held[tuple(place)] = pieces[piece].at[index] if index else pieces[piece]
        for k in range(KT):
            cols = slice(k * STEP, (k + 1) * STEP)
            block = jnp.concatenate(
                [held[dy, g, h][:, cols] for dy in range(NY) for g in range(NC) for h in range(2)]
            )
            term = lax.dot_general(
                block, amps[n * KT + k], (((1,), (1,)), ((), ())), preferred_element_type=jnp.float32
            )
            if n == k == 0:
                total[...] = term
            else:
                total[...] += term

    spot = lax.axis_index("blk")
    y, x, c = spot // (NX * NC), (spot // NC) % NX, spot % NC
    z = lax.axis_index("row") // NH
    for dz in range(NZ):
        dy = (z + dz + NY - y) % NY
        for core in range(NC):
            here = (dy * NC + (core + NC - c) % NC) * SB
            there = ((((z + dz) % NZ) * NX + (x + e) % NX) * NC + core) * SB
            there = pl.ds(pl.multiple_of(there, SB), SB)
            outs[dz][core * SB : (core + 1) * SB, :] = total[
                pl.ds(pl.multiple_of(here, SB), SB), :
            ] + jnp.concatenate([cycle[n, there, :] for n in range(cycle.shape[0])], axis=1)


def ladder(e, amplitudes, cycle, before, pieces):
    places = [(n, *place) for n, (_, held) in enumerate(pieces) for place in held]
    places = [(n, index, slot, dy % NY, g, h) for n, index, slot, dy, g, h in places]
    rows, q = amplitudes.shape[1], NY * NC * SB
    out = jax.ShapeDtypeStruct((q // NZ, rows), jnp.float32)
    return pl.pallas_call(
        functools.partial(ladder_kernel, places, e, len(pieces)),
        out_shape=(out,) * NZ + (jax.ShapeDtypeStruct((8, 128), jnp.float32),),
        in_specs=[pl.BlockSpec(memory_space=pltpu.VMEM)] * (3 + len(pieces)),
        out_specs=[pl.BlockSpec(memory_space=pltpu.VMEM)] * (NZ + 1),
        scratch_shapes=[pltpu.VMEM((q, rows), jnp.float32)],
        compiler_params=pltpu.CompilerParams(vmem_limit_bytes=24 * MIB),
        cost_estimate=pl.CostEstimate(
            flops=2 * q * rows * 2 * TILE, bytes_accessed=2 * q * 2 * TILE, transcendentals=0
        ),
        name="ladder",
    )(amplitudes, cycle, before, *[array for array, _ in pieces])


def pack_kernel(*refs):
    *blocks, out = refs
    for e, block in enumerate(blocks):
        for n in range(block.shape[0] // HALF):
            at = (e * (block.shape[0] // HALF) + n) * block.shape[1]
            out[0, :, at : at + block.shape[1]] = block[n * HALF : (n + 1) * HALF, :]


def pack(*blocks):
    return pl.pallas_call(
        pack_kernel,
        out_shape=jax.ShapeDtypeStruct((1, HALF, TILE), blocks[0].dtype),
        in_specs=[pl.BlockSpec(memory_space=pltpu.VMEM)] * len(blocks),
        out_specs=pl.BlockSpec(memory_space=pltpu.VMEM),
        compiler_params=pltpu.CompilerParams(vmem_limit_bytes=4 * MIB),
        name="pack",
    )(*blocks)


def cycle_kernel(places, width, slab_amps, token, *refs):
    blocks, out, turned, rows_of = refs[:-3], refs[-3], refs[-2], refs[-1]
    k_local, i_local, ac = slab_amps.shape
    a_all, per = ac // SB, rows_of.shape[-1] // SB
    for part in range(k_local // per):
        held = [slab_amps[part * per + n].astype(jnp.float32) for n in range(per)]
        for a in range(a_all):
            row = jnp.concatenate([k[:, a * SB : (a + 1) * SB] for k in held], axis=1)
            rows_of[part, pl.ds(a, i_local, stride=a_all), :] = row
    slab = jnp.concatenate([rows_of[part] for part in range(k_local // per)], axis=1).astype(jnp.bfloat16)
    spot = lax.axis_index("blk")
    y, x, c = spot // (NX * NC), (spot // NC) % NX, spot % NC
    pairs, depth = slab.shape
    for piece, index, half, dy, e, g in places:
        tiles = []
        for n in range(depth // HALF):
            at = (half * (depth // HALF) + n) * width
            tiles.append(blocks[piece][(*index, slice(None), slice(at, at + width))])
        term = jnp.dot(slab, jnp.concatenate(tiles), preferred_element_type=jnp.float32)
        block = ((y + dy) % NY * NX + (x + e) % NX) * NC + (c + g) % NC
        turned[pl.ds(pl.multiple_of(block * width, width), width), :] = term.T
    for b in range(SB):
        rows = turned[pl.ds(b, OW, stride=SB), :].T
        for i in range(0, pairs // a_all, 2):
            both = [rows[at * a_all : (at + 1) * a_all] for at in (i, i + 1)]
            out[i // 2, pl.ds(b, a_all, stride=SB), :] = jnp.concatenate(both, axis=1)


def cycle_sums(slab_amplitudes, pieces, token):
    k_local, i_local, ac = slab_amplitudes.shape
    a_all, depth = ac // SB, k_local * SB
    arrays = list({id(array): array for array, *_ in pieces}.values())
    order = [id(array) for array in arrays]
    places = [(order.index(id(array)), index, half, dy % NY, e, g) for array, index, half, dy, e, g in pieces]
    width = OW * SB // (NY * NX * NC)
    return pl.pallas_call(
        functools.partial(cycle_kernel, places, width),
        out_shape=jax.ShapeDtypeStruct((i_local // 2, a_all * SB, 2 * OW), jnp.float32),
        in_specs=[pl.BlockSpec(memory_space=pltpu.VMEM)] * (2 + len(arrays)),
        out_specs=pl.BlockSpec(memory_space=pltpu.VMEM),
        scratch_shapes=[
            pltpu.VMEM((OW * SB, i_local * a_all), jnp.float32),
            pltpu.VMEM((depth // LANES, i_local * a_all, LANES), jnp.float32),
        ],
        compiler_params=pltpu.CompilerParams(vmem_limit_bytes=16 * MIB),
        cost_estimate=pl.CostEstimate(
            flops=2 * i_local * a_all * depth * OW * SB, bytes_accessed=8 * MIB, transcendentals=0
        ),
        name="cycle",
    )(slab_amplitudes, token, *arrays)


def sum_along_z(parts):
    total = parts[0]
    for dz in range(1, NZ):
        total = total + move_row(parts[dz], dz=dz)
    return total


def per_device(amplitudes, integrals, live_pairs, slab_amplitudes, cycle_integrals):
    def swap(*arrays):
        return (jnp.concatenate(arrays), move(jnp.concatenate(arrays), dc=1))

    own = pick_live(live_pairs, integrals.T)
    below, above, beside = move(own, dy=1), move(own, dy=-1), move(own, dx=1)
    cycle_beside, cycle_far = move(cycle_integrals, dx=1), move(cycle_integrals, dy=2)
    live_amps, token = load_live(live_pairs, amplitudes, own)
    cycle_beside, token = together(cycle_beside, token)
    pair = pack(cycle_integrals, cycle_beside)
    below, above, beside, cycle_far, pair, token = together(below, above, beside, cycle_far, pair, token)

    far = pack(cycle_far)
    from_below = move(jnp.concatenate([below[0:2], beside[0:2], pair]), dy=1)
    from_above = move(jnp.concatenate([above[2:4], beside[0:2], pair]), dy=-1)
    across = move(jnp.concatenate([below[2:4], above[2:4], far]), dx=1)
    hop = swap(own, below, above, beside, pair, far)

    from_below, from_above, across = together(from_below, from_above, across)
    last_below = move(jnp.concatenate([from_below[2:3], across[0:1]]), dy=1)
    last_above = move(jnp.concatenate([from_above[3:4], across[3:4]]), dy=-1)
    hop_near = swap(from_below[0:2], from_above[0:2], from_below[4:5], from_above[4:5], across[4:5])
    hop_far = swap(from_below[2:4], from_above[2:4], across[0:4])

    blocks = []
    for g in range(NC):
        for e in range(2):
            blocks += [(hop[g], (16,), e, 0, e, g), (hop_near[g], (4,), e, -1, e, g), (hop_near[g], (5,), e, 1, e, g)]
        blocks += [(hop[g], (17,), 0, 2, 0, g), (hop_near[g], (6,), 0, 2, 1, g)]
    cycle = cycle_sums(slab_amplitudes, blocks, token)
    token, hop_1 = together(token, hop_far[1])
    hop_far = (hop_far[0], hop_1)

    halves = [(h, n) for h in range(2) for n in range(2)]
    near = []
    for g in range(NC):
        places = [((4 * at + 2 * h + n,), n, dy, g, h) for at, dy in enumerate((0, -1, 1)) for h, n in halves]
        near += [(hop[g], places), (hop_near[g], [((2 * h + n,), n, 2, g, h) for h, n in halves])]
    *near, token = ladder(0, live_amps, cycle, token, near)
    near = sum_along_z(near)

    last_below, last_above, token = together(last_below, last_above, token)
    far = []
    for g in range(NC):
        places = [((2 * at + n,), n, dy, g, 0) for at, dy in enumerate((-1, 1)) for n in range(2)]
        places += [((4 + 2 * at + n,), n, dy, g, 1) for at, dy in enumerate((-1, 1)) for n in range(2)]
        far += [(hop[g], [((12 + 2 * h + n,), n, 0, g, h) for h, n in halves]), (hop_far[g], places)]
    for g, both in enumerate(swap(last_below, last_above)):
        far.append((both, [((2 * n + h,), n, 2, g, h) for h, n in halves]))
    far = sum_along_z(ladder(1, live_amps, cycle, token, far)[:NZ])

    mine = lax.axis_index("row") % NH == (lax.axis_index("blk") // NC) % NX
    total = jnp.where(mine, near, far) + move_row(jnp.where(mine, far, near), dx=1)
    return total.astype(jnp.bfloat16).T


def solution(mesh):
    return jax.shard_map(
        per_device,
        mesh=mesh,
        in_specs=(
            P("blk", "row"),
            P("row", "blk"),
            P("row"),
            P("row", "blk", None),
            P("row", "blk"),
        ),
        out_specs=P("blk", "row"),
        check_vma=False,
    )
```

```python
import functools

import jax
import jax.numpy as jnp
from jax import lax
from jax.experimental import pallas as pl
from jax.experimental.pallas import tpu as pltpu
from jax.sharding import PartitionSpec as P

OW = 64
TS = 64
SB = 32
TILE = TS * TS
NY, NX, NC = 4, 2, 2
NZ, NH = 4, 2
HALF = SB // 2
STEP = 1024
KT = TILE // STEP
MIB = 1 << 20
LANES = 128


def blk_moves(dy, dx, dc):
    spots = [(y, x, c) for y in range(NY) for x in range(NX) for c in range(NC)]
    index = lambda y, x, c: (y * NX + x) * NC + c
    return [(index(y, x, c), index(y ^ dy, x ^ dx, c ^ dc)) for y, x, c in spots]


def row_moves(dz, dx):
    spots = [(z, x) for z in range(NZ) for x in range(NH)]
    return [(z * NH + x, (z ^ dz) * NH + (x ^ dx)) for z, x in spots]


def move(value, dy=0, dx=0, dc=0):
    return lax.ppermute(value, "blk", blk_moves(dy, dx, dc))


def move_row(value, dz=0, dx=0):
    return lax.ppermute(value, "row", row_moves(dz, dx))


def together(*values):
    return lax.optimization_barrier(values)


def live_slot(live, n):
    if n == 0:
        return jnp.where(live[0] == 1, 0, jnp.where(live[1] == 1, 1, 2))
    return jnp.where(live[3] == 1, 3, jnp.where(live[2] == 1, 2, 1))


def pick_kernel(live, columns, out, sems):
    copies = []
    for n in range(2):
        start = pl.multiple_of(live_slot(live, n) * TILE, TILE)
        for h in range(2):
            source = columns.at[pl.ds(h * HALF, HALF), pl.ds(start, TILE)]
            copies.append(pltpu.make_async_copy(source, out.at[2 * h + n], sems.at[n, h]))
    for copy in copies:
        copy.start()
    for copy in copies:
        copy.wait()


def pick_live(live_pairs, columns):
    return pl.pallas_call(
        pick_kernel,
        out_shape=jax.ShapeDtypeStruct((4, HALF, TILE), columns.dtype),
        in_specs=[pl.BlockSpec(memory_space=pltpu.SMEM), pl.BlockSpec(memory_space=pltpu.HBM)],
        out_specs=pl.BlockSpec(memory_space=pltpu.VMEM),
        scratch_shapes=[pltpu.SemaphoreType.DMA((2, 2))],
        compiler_params=pltpu.CompilerParams(vmem_limit_bytes=4 * MIB),
        name="pick_live",
    )(live_pairs, columns)


def load_kernel(live, amps, after, out, token, sems):
    token[...] = jnp.zeros_like(token)
    copies = []
    for n in range(2):
        for k in range(KT):
            start = pl.multiple_of(live_slot(live, n) * TILE + k * STEP, STEP)
            at = n * KT + k
            copies.append(pltpu.make_async_copy(amps.at[:, pl.ds(start, STEP)], out.at[at], sems.at[at]))
    for copy in copies:
        copy.start()
    for copy in copies:
        copy.wait()


def load_live(live_pairs, amplitudes, after):
    rows = amplitudes.shape[0]
    return pl.pallas_call(
        load_kernel,
        out_shape=(
            jax.ShapeDtypeStruct((2 * KT, rows, STEP), amplitudes.dtype),
            jax.ShapeDtypeStruct((8, 128), jnp.float32),
        ),
        in_specs=[pl.BlockSpec(memory_space=pltpu.SMEM)] + [pl.BlockSpec(memory_space=pl.ANY)] * 2,
        out_specs=(pl.BlockSpec(memory_space=pltpu.VMEM),) * 2,
        scratch_shapes=[pltpu.SemaphoreType.DMA((2 * KT,))],
        compiler_params=pltpu.CompilerParams(vmem_limit_bytes=40 * MIB),
        name="load_live",
    )(live_pairs, amplitudes, after)


def ladder_kernel(places, e, count, amps, cycle, before, *refs):
    pieces, outs, (token, total) = refs[:count], refs[count : count + NZ], refs[count + NZ :]
    token[...] = jnp.zeros_like(token)
    for n in range(2):
        held = {}
        for piece, index, slot, *place in places:
            if slot == n:
                held[tuple(place)] = pieces[piece].at[index] if index else pieces[piece]
        for k in range(KT):
            cols = slice(k * STEP, (k + 1) * STEP)
            block = jnp.concatenate(
                [held[dy, g, h][:, cols] for dy in range(NY) for g in range(NC) for h in range(2)]
            )
            term = lax.dot_general(
                block, amps[n * KT + k], (((1,), (1,)), ((), ())), preferred_element_type=jnp.float32
            )
            if n == k == 0:
                total[...] = term
            else:
                total[...] += term

    spot = lax.axis_index("blk")
    y, x, c = spot // (NX * NC), (spot // NC) % NX, spot % NC
    z = lax.axis_index("row") // NH
    for dz in range(NZ):
        dy = (z ^ dz) ^ y
        for core in range(NC):
            here = (dy * NC + (c ^ core)) * SB
            there = (((z ^ dz) * NX + (x ^ e)) * NC + core) * SB
            there = pl.ds(pl.multiple_of(there, SB), SB)
            outs[dz][core * SB : (core + 1) * SB, :] = total[
                pl.ds(pl.multiple_of(here, SB), SB), :
            ] + jnp.concatenate([cycle[n, there, :] for n in range(cycle.shape[0])], axis=1)


def ladder(e, amplitudes, cycle, before, pieces):
    places = [(n, *place) for n, (_, held) in enumerate(pieces) for place in held]
    rows, q = amplitudes.shape[1], NY * NC * SB
    out = jax.ShapeDtypeStruct((q // NZ, rows), jnp.float32)
    return pl.pallas_call(
        functools.partial(ladder_kernel, places, e, len(pieces)),
        out_shape=(out,) * NZ + (jax.ShapeDtypeStruct((8, 128), jnp.float32),),
        in_specs=[pl.BlockSpec(memory_space=pltpu.VMEM)] * (3 + len(pieces)),
        out_specs=[pl.BlockSpec(memory_space=pltpu.VMEM)] * (NZ + 1),
        scratch_shapes=[pltpu.VMEM((q, rows), jnp.float32)],
        compiler_params=pltpu.CompilerParams(vmem_limit_bytes=24 * MIB),
        cost_estimate=pl.CostEstimate(
            flops=2 * q * rows * 2 * TILE, bytes_accessed=2 * q * 2 * TILE, transcendentals=0
        ),
        name="ladder",
    )(amplitudes, cycle, before, *[array for array, _ in pieces])


def pack_kernel(*refs):
    *blocks, out = refs
    for e, block in enumerate(blocks):
        for n in range(block.shape[0] // HALF):
            at = (e * (block.shape[0] // HALF) + n) * block.shape[1]
            out[0, :, at : at + block.shape[1]] = block[n * HALF : (n + 1) * HALF, :]


def pack(*blocks):
    return pl.pallas_call(
        pack_kernel,
        out_shape=jax.ShapeDtypeStruct((1, HALF, TILE), blocks[0].dtype),
        in_specs=[pl.BlockSpec(memory_space=pltpu.VMEM)] * len(blocks),
        out_specs=pl.BlockSpec(memory_space=pltpu.VMEM),
        compiler_params=pltpu.CompilerParams(vmem_limit_bytes=4 * MIB),
        name="pack",
    )(*blocks)


def cycle_kernel(places, width, slab_amps, token, *refs):
    blocks, out, turned, rows_of = refs[:-3], refs[-3], refs[-2], refs[-1]
    k_local, i_local, ac = slab_amps.shape
    a_all, per = ac // SB, rows_of.shape[-1] // SB
    for part in range(k_local // per):
        held = [slab_amps[part * per + n].astype(jnp.float32) for n in range(per)]
        for a in range(a_all):
            row = jnp.concatenate([k[:, a * SB : (a + 1) * SB] for k in held], axis=1)
            rows_of[part, pl.ds(a, i_local, stride=a_all), :] = row
    slab = jnp.concatenate([rows_of[part] for part in range(k_local // per)], axis=1).astype(jnp.bfloat16)
    spot = lax.axis_index("blk")
    y, x, c = spot // (NX * NC), (spot // NC) % NX, spot % NC
    pairs, depth = slab.shape
    for piece, index, half, dy, e, g in places:
        tiles = []
        for n in range(depth // HALF):
            at = (half * (depth // HALF) + n) * width
            tiles.append(blocks[piece][(*index, slice(None), slice(at, at + width))])
        term = jnp.dot(slab, jnp.concatenate(tiles), preferred_element_type=jnp.float32)
        block = ((y ^ dy) * NX + (x ^ e)) * NC + (c ^ g)
        turned[pl.ds(pl.multiple_of(block * width, width), width), :] = term.T
    for b in range(SB):
        rows = turned[pl.ds(b, OW, stride=SB), :].T
        for i in range(0, pairs // a_all, 2):
            both = [rows[at * a_all : (at + 1) * a_all] for at in (i, i + 1)]
            out[i // 2, pl.ds(b, a_all, stride=SB), :] = jnp.concatenate(both, axis=1)


def cycle_sums(slab_amplitudes, pieces, token):
    k_local, i_local, ac = slab_amplitudes.shape
    a_all, depth = ac // SB, k_local * SB
    arrays = list({id(array): array for array, *_ in pieces}.values())
    order = [id(array) for array in arrays]
    places = [(order.index(id(array)), index, half, dy, e, g) for array, index, half, dy, e, g in pieces]
    width = OW * SB // (NY * NX * NC)
    return pl.pallas_call(
        functools.partial(cycle_kernel, places, width),
        out_shape=jax.ShapeDtypeStruct((i_local // 2, a_all * SB, 2 * OW), jnp.float32),
        in_specs=[pl.BlockSpec(memory_space=pltpu.VMEM)] * (2 + len(arrays)),
        out_specs=pl.BlockSpec(memory_space=pltpu.VMEM),
        scratch_shapes=[
            pltpu.VMEM((OW * SB, i_local * a_all), jnp.float32),
            pltpu.VMEM((depth // LANES, i_local * a_all, LANES), jnp.float32),
        ],
        compiler_params=pltpu.CompilerParams(vmem_limit_bytes=16 * MIB),
        cost_estimate=pl.CostEstimate(
            flops=2 * i_local * a_all * depth * OW * SB, bytes_accessed=8 * MIB, transcendentals=0
        ),
        name="cycle",
    )(slab_amplitudes, token, *arrays)


def sum_along_z(parts):
    total = parts[0]
    for dz in (1, 3, 2):
        total = total + move_row(parts[dz], dz=dz)
    return total


def per_device(amplitudes, integrals, live_pairs, slab_amplitudes, cycle_integrals):
    def swap(*arrays):
        return (jnp.concatenate(arrays), move(jnp.concatenate(arrays), dc=1))

    own = pick_live(live_pairs, integrals.T)
    below, above, beside = move(own, dy=1), move(own, dy=3), move(own, dx=1)
    cycle_beside, cycle_far = move(cycle_integrals, dx=1), move(cycle_integrals, dy=2)
    live_amps, token = load_live(live_pairs, amplitudes, own)
    cycle_beside, token = together(cycle_beside, token)
    pair = pack(cycle_integrals, cycle_beside)
    beside, above, below, cycle_far, pair, token = together(beside, above, below, cycle_far, pair, token)

    far = pack(cycle_far)
    from_above = move(jnp.concatenate([below[0:2], beside[0:2], pair]), dy=3)
    from_below = move(jnp.concatenate([above[2:4], beside[0:2], pair]), dy=1)
    across = move(jnp.concatenate([below[2:4], above[2:4], far]), dx=1)
    hop = swap(own, below, above, beside, pair, far)

    from_above, from_below, across = together(from_above, from_below, across)
    last_above = move(jnp.concatenate([from_below[2:3], across[0:1]]), dy=3)
    last_below = move(jnp.concatenate([from_above[3:4], across[3:4]]), dy=1)
    hop_near = swap(from_above[0:2], from_below[0:2], from_above[4:5], from_below[4:5], across[4:5])
    hop_far = swap(from_above[2:4], from_below[2:4], across[0:4])

    blocks = []
    for g in range(NC):
        for e in range(2):
            blocks += [(hop[g], (16,), e, 0, e, g), (hop_near[g], (4,), e, 3, e, g), (hop_near[g], (5,), e, 1, e, g)]
        blocks += [(hop[g], (17,), 0, 2, 0, g), (hop_near[g], (6,), 0, 2, 1, g)]
    cycle = cycle_sums(slab_amplitudes, blocks, token)
    token, hop_1 = together(token, hop_far[1])
    hop_far = (hop_far[0], hop_1)

    halves = [(h, n) for h in range(2) for n in range(2)]
    near = []
    for g in range(NC):
        places = [((4 * at + 2 * h + n,), n, dy, g, h) for at, dy in enumerate((0, 1, 3)) for h, n in halves]
        near += [(hop[g], places), (hop_near[g], [((2 * h + n,), n, 2, g, h) for h, n in halves])]
    *near, token = ladder(0, live_amps, cycle, token, near)
    near = sum_along_z(near)

    last_above, last_below, token = together(last_above, last_below, token)
    far = []
    for g in range(NC):
        places = [((2 * at + n,), n, dy, g, 0) for at, dy in enumerate((3, 1)) for n in range(2)]
        places += [((4 + 2 * at + n,), n, dy, g, 1) for at, dy in enumerate((1, 3)) for n in range(2)]
        far += [(hop[g], [((12 + 2 * h + n,), n, 0, g, h) for h, n in halves]), (hop_far[g], places)]
    for g, both in enumerate(swap(last_above, last_below)):
        far.append((both, [((2 * n + h,), n, 2, g, h) for h, n in halves]))
    far = sum_along_z(ladder(1, live_amps, cycle, token, far)[:NZ])

    mine = lax.axis_index("row") % NH == (lax.axis_index("blk") // NC) % NX
    total = jnp.where(mine, near, far) + move_row(jnp.where(mine, far, near), dx=1)
    return total.astype(jnp.bfloat16).T


def solution(mesh):
    return jax.shard_map(
        per_device,
        mesh=mesh,
        in_specs=(
            P("blk", "row"),
            P("row", "blk"),
            P("row"),
            P("row", "blk", None),
            P("row", "blk"),
        ),
        out_specs=P("blk", "row"),
        check_vma=False,
    )
```

```python
import functools

import jax
import jax.numpy as jnp
from jax import lax
from jax.experimental import pallas as pl
from jax.experimental.pallas import tpu as pltpu
from jax.sharding import PartitionSpec as P

OW = 64
TS = 64
SB = 32
TILE = TS * TS
NY, NX, NC = 4, 2, 2
NZ, NH = 4, 2
HALF = SB // 2
STEP = 1024
KT = TILE // STEP
MIB = 1 << 20
LANES = 128


def blk_moves(dy, dx, dc):
    spots = [(y, x, c) for y in range(NY) for x in range(NX) for c in range(NC)]
    index = lambda y, x, c: (y * NX + x) * NC + c
    return [(index(y, x, c), index(y ^ dy, x ^ dx, c ^ dc)) for y, x, c in spots]


def row_moves(dz, dx):
    spots = [(z, x) for z in range(NZ) for x in range(NH)]
    return [(z * NH + x, (z ^ dz) * NH + (x ^ dx)) for z, x in spots]


def move(value, dy=0, dx=0, dc=0):
    return lax.ppermute(value, "blk", blk_moves(dy, dx, dc))


def move_row(value, dz=0, dx=0):
    return lax.ppermute(value, "row", row_moves(dz, dx))


def together(*values):
    return lax.optimization_barrier(values)


def live_slot(live, n):
    if n == 0:
        return jnp.where(live[0] == 1, 0, jnp.where(live[1] == 1, 1, 2))
    return jnp.where(live[3] == 1, 3, jnp.where(live[2] == 1, 2, 1))


def pick_kernel(live, columns, out, sems):
    copies = []
    for n in range(2):
        start = pl.multiple_of(live_slot(live, n) * TILE, TILE)
        for h in range(2):
            source = columns.at[pl.ds(h * HALF, HALF), pl.ds(start, TILE)]
            copies.append(pltpu.make_async_copy(source, out.at[2 * h + n], sems.at[n, h]))
    for copy in copies:
        copy.start()
    for copy in copies:
        copy.wait()


def pick_live(live_pairs, columns):
    return pl.pallas_call(
        pick_kernel,
        out_shape=jax.ShapeDtypeStruct((4, HALF, TILE), columns.dtype),
        in_specs=[pl.BlockSpec(memory_space=pltpu.SMEM), pl.BlockSpec(memory_space=pltpu.HBM)],
        out_specs=pl.BlockSpec(memory_space=pltpu.VMEM),
        scratch_shapes=[pltpu.SemaphoreType.DMA((2, 2))],
        compiler_params=pltpu.CompilerParams(vmem_limit_bytes=4 * MIB),
        name="pick_live",
    )(live_pairs, columns)


def load_kernel(live, amps, after, out, token, sems):
    token[...] = jnp.zeros_like(token)
    copies = []
    for n in range(2):
        for k in range(KT):
            start = pl.multiple_of(live_slot(live, n) * TILE + k * STEP, STEP)
            at = n * KT + k
            copies.append(pltpu.make_async_copy(amps.at[:, pl.ds(start, STEP)], out.at[at], sems.at[at]))
    for copy in copies:
        copy.start()
    for copy in copies:
        copy.wait()


def load_live(live_pairs, amplitudes, after):
    rows = amplitudes.shape[0]
    return pl.pallas_call(
        load_kernel,
        out_shape=(
            jax.ShapeDtypeStruct((2 * KT, rows, STEP), amplitudes.dtype),
            jax.ShapeDtypeStruct((8, 128), jnp.float32),
        ),
        in_specs=[pl.BlockSpec(memory_space=pltpu.SMEM)] + [pl.BlockSpec(memory_space=pl.ANY)] * 2,
        out_specs=(pl.BlockSpec(memory_space=pltpu.VMEM),) * 2,
        scratch_shapes=[pltpu.SemaphoreType.DMA((2 * KT,))],
        compiler_params=pltpu.CompilerParams(vmem_limit_bytes=40 * MIB),
        name="load_live",
    )(live_pairs, amplitudes, after)


def ladder_kernel(places, e, count, amps, cycle, before, *refs):
    pieces, outs, (token, total) = refs[:count], refs[count:-2], refs[-2:]
    token[...] = jnp.zeros_like(token)
    for n in range(2):
        held = {}
        for piece, index, slot, *place in places:
            if slot == n:
                held[tuple(place)] = pieces[piece].at[index] if index else pieces[piece]
        for k in range(KT):
            cols = slice(k * STEP, (k + 1) * STEP)
            block = jnp.concatenate(
                [held[dy, g, h][:, cols] for dy in range(NY) for g in range(NC) for h in range(2)]
            )
            term = lax.dot_general(
                block, amps[n * KT + k], (((1,), (1,)), ((), ())), preferred_element_type=jnp.float32
            )
            if n == k == 0:
                total[...] = term
            else:
                total[...] += term

    spot = lax.axis_index("blk")
    y, x, c = spot // (NX * NC), (spot // NC) % NX, spot % NC
    z = lax.axis_index("row") // NH
    for dz in range(NZ):
        dy = (z ^ dz) ^ y
        for core in range(NC):
            here = (dy * NC + (c ^ core)) * SB
            there = (((z ^ dz) * NX + (x ^ e)) * NC + core) * SB
            there = pl.ds(pl.multiple_of(there, SB), SB)
            rows = slice(core * SB, (core + 1) * SB)
            value = total[pl.ds(pl.multiple_of(here, SB), SB), :] + jnp.concatenate(
                [cycle[n, there, :] for n in range(cycle.shape[0])], axis=1
            )
            if dz == 2 and len(outs) > NZ:
                mine = x == lax.axis_index("row") % NH
                outs[2][rows, :] = jnp.where(mine, before[rows, :], value)
                outs[NZ][rows, :] = jnp.where(mine, value, before[rows, :])
            else:
                outs[dz][rows, :] = value


def ladder(e, amplitudes, cycle, before, pieces, exchange=False):
    places = [(n, *place) for n, (_, held) in enumerate(pieces) for place in held]
    rows, q = amplitudes.shape[1], NY * NC * SB
    out = jax.ShapeDtypeStruct((q // NZ, rows), jnp.float32)
    return pl.pallas_call(
        functools.partial(ladder_kernel, places, e, len(pieces)),
        out_shape=(out,) * (NZ + exchange) + (jax.ShapeDtypeStruct((8, 128), jnp.float32),),
        in_specs=[pl.BlockSpec(memory_space=pltpu.VMEM)] * (3 + len(pieces)),
        out_specs=[pl.BlockSpec(memory_space=pltpu.VMEM)] * (NZ + exchange + 1),
        scratch_shapes=[pltpu.VMEM((q, rows), jnp.float32)],
        compiler_params=pltpu.CompilerParams(vmem_limit_bytes=24 * MIB),
        cost_estimate=pl.CostEstimate(
            flops=2 * q * rows * 2 * TILE, bytes_accessed=2 * q * 2 * TILE, transcendentals=0
        ),
        name="ladder",
    )(amplitudes, cycle, before, *[array for array, _ in pieces])


def pack_kernel(*refs):
    *blocks, out = refs
    for e, block in enumerate(blocks):
        for n in range(block.shape[0] // HALF):
            at = (e * (block.shape[0] // HALF) + n) * block.shape[1]
            out[0, :, at : at + block.shape[1]] = block[n * HALF : (n + 1) * HALF, :]


def pack(*blocks):
    return pl.pallas_call(
        pack_kernel,
        out_shape=jax.ShapeDtypeStruct((1, HALF, TILE), blocks[0].dtype),
        in_specs=[pl.BlockSpec(memory_space=pltpu.VMEM)] * len(blocks),
        out_specs=pl.BlockSpec(memory_space=pltpu.VMEM),
        compiler_params=pltpu.CompilerParams(vmem_limit_bytes=4 * MIB),
        name="pack",
    )(*blocks)


def cycle_kernel(places, width, slab_amps, token, *refs):
    blocks, out, turned, rows_of = refs[:-3], refs[-3], refs[-2], refs[-1]
    k_local, i_local, ac = slab_amps.shape
    a_all, per = ac // SB, rows_of.shape[-1] // SB
    for part in range(k_local // per):
        held = [slab_amps[part * per + n].astype(jnp.float32) for n in range(per)]
        for a in range(a_all):
            row = jnp.concatenate([k[:, a * SB : (a + 1) * SB] for k in held], axis=1)
            rows_of[part, pl.ds(a, i_local, stride=a_all), :] = row
    slab = jnp.concatenate([rows_of[part] for part in range(k_local // per)], axis=1).astype(jnp.bfloat16)
    spot = lax.axis_index("blk")
    y, x, c = spot // (NX * NC), (spot // NC) % NX, spot % NC
    pairs, depth = slab.shape
    for piece, index, half, dy, e, g in places:
        tiles = []
        for n in range(depth // HALF):
            at = (half * (depth // HALF) + n) * width
            tiles.append(blocks[piece][(*index, slice(None), slice(at, at + width))])
        term = jnp.dot(slab, jnp.concatenate(tiles), preferred_element_type=jnp.float32)
        block = ((y ^ dy) * NX + (x ^ e)) * NC + (c ^ g)
        turned[pl.ds(pl.multiple_of(block * width, width), width), :] = term.T
    for b in range(SB):
        rows = turned[pl.ds(b, OW, stride=SB), :].T
        for i in range(0, pairs // a_all, 2):
            both = [rows[at * a_all : (at + 1) * a_all] for at in (i, i + 1)]
            out[i // 2, pl.ds(b, a_all, stride=SB), :] = jnp.concatenate(both, axis=1)


def cycle_sums(slab_amplitudes, pieces, token):
    k_local, i_local, ac = slab_amplitudes.shape
    a_all, depth = ac // SB, k_local * SB
    arrays = list({id(array): array for array, *_ in pieces}.values())
    order = [id(array) for array in arrays]
    places = [(order.index(id(array)), index, half, dy, e, g) for array, index, half, dy, e, g in pieces]
    width = OW * SB // (NY * NX * NC)
    return pl.pallas_call(
        functools.partial(cycle_kernel, places, width),
        out_shape=jax.ShapeDtypeStruct((i_local // 2, a_all * SB, 2 * OW), jnp.float32),
        in_specs=[pl.BlockSpec(memory_space=pltpu.VMEM)] * (2 + len(arrays)),
        out_specs=pl.BlockSpec(memory_space=pltpu.VMEM),
        scratch_shapes=[
            pltpu.VMEM((OW * SB, i_local * a_all), jnp.float32),
            pltpu.VMEM((depth // LANES, i_local * a_all, LANES), jnp.float32),
        ],
        compiler_params=pltpu.CompilerParams(vmem_limit_bytes=16 * MIB),
        cost_estimate=pl.CostEstimate(
            flops=2 * i_local * a_all * depth * OW * SB, bytes_accessed=8 * MIB, transcendentals=0
        ),
        name="cycle",
    )(slab_amplitudes, token, *arrays)


def sum_beside(parts):
    return parts[0] + move_row(parts[1], dz=1) + move_row(parts[3], dz=3)


def per_device(amplitudes, integrals, live_pairs, slab_amplitudes, cycle_integrals):
    def swap(*arrays):
        return (jnp.concatenate(arrays), move(jnp.concatenate(arrays), dc=1))

    own = pick_live(live_pairs, integrals.T)
    below, above, beside = move(own, dy=1), move(own, dy=3), move(own, dx=1)
    cycle_beside, cycle_far = move(cycle_integrals, dx=1), move(cycle_integrals, dy=2)
    live_amps, token = load_live(live_pairs, amplitudes, own)
    cycle_beside, token = together(cycle_beside, token)
    pair = pack(cycle_integrals, cycle_beside)
    beside, above, below, cycle_far, pair, token = together(beside, above, below, cycle_far, pair, token)

    far = pack(cycle_far)
    from_above = move(jnp.concatenate([below[0:2], beside[0:2], pair]), dy=3)
    from_below = move(jnp.concatenate([above[2:4], beside[0:2], pair]), dy=1)
    across = move(jnp.concatenate([below[2:4], above[2:4], far]), dx=1)
    hop = swap(own, below, above, beside, pair, far)

    from_above, from_below, across = together(from_above, from_below, across)
    last_above = move(jnp.concatenate([from_below[2:3], across[0:1]]), dy=3)
    last_below = move(jnp.concatenate([from_above[3:4], across[3:4]]), dy=1)
    hop_near = swap(from_above[0:2], from_below[0:2], from_above[4:5], from_below[4:5], across[4:5])
    hop_far = swap(from_above[2:4], from_below[2:4], across[0:4])

    blocks = []
    for g in range(NC):
        for e in range(2):
            blocks += [(hop[g], (16,), e, 0, e, g), (hop_near[g], (4,), e, 3, e, g), (hop_near[g], (5,), e, 1, e, g)]
        blocks += [(hop[g], (17,), 0, 2, 0, g), (hop_near[g], (6,), 0, 2, 1, g)]
    cycle = cycle_sums(slab_amplitudes, blocks, token)
    token, hop_1 = together(token, hop_far[1])
    hop_far = (hop_far[0], hop_1)

    halves = [(h, n) for h in range(2) for n in range(2)]
    near = []
    for g in range(NC):
        places = [((4 * at + 2 * h + n,), n, dy, g, h) for at, dy in enumerate((0, 1, 3)) for h, n in halves]
        near += [(hop[g], places), (hop_near[g], [((2 * h + n,), n, 2, g, h) for h, n in halves])]
    *near, token = ladder(0, live_amps, cycle, token, near)
    near_sum = sum_beside(near)

    last_above, last_below, before = together(last_above, last_below, near[2])
    far = []
    for g in range(NC):
        places = [((2 * at + n,), n, dy, g, 0) for at, dy in enumerate((3, 1)) for n in range(2)]
        places += [((4 + 2 * at + n,), n, dy, g, 1) for at, dy in enumerate((1, 3)) for n in range(2)]
        far += [(hop[g], [((12 + 2 * h + n,), n, 0, g, h) for h, n in halves]), (hop_far[g], places)]
    for g, both in enumerate(swap(last_above, last_below)):
        far.append((both, [((2 * n + h,), n, 2, g, h) for h, n in halves]))
    *far, other, _ = ladder(1, live_amps, cycle, before, far, exchange=True)
    far_sum = sum_beside(far)

    mine = lax.axis_index("row") % NH == (lax.axis_index("blk") // NC) % NX
    total = jnp.where(mine, near_sum, far_sum) + move_row(jnp.where(mine, far_sum, near_sum), dx=1)
    total = total + move_row(other, dz=2, dx=1) + move_row(far[2], dz=2)
    return total.astype(jnp.bfloat16).T


def solution(mesh):
    return jax.shard_map(
        per_device,
        mesh=mesh,
        in_specs=(
            P("blk", "row"),
            P("row", "blk"),
            P("row"),
            P("row", "blk", None),
            P("row", "blk"),
        ),
        out_specs=P("blk", "row"),
        check_vma=False,
    )
```

```python
import functools

import jax
import jax.numpy as jnp
from jax import lax
from jax.experimental import pallas as pl
from jax.experimental.pallas import tpu as pltpu
from jax.sharding import PartitionSpec as P

OW = 64
TS = 64
SB = 32
TILE = TS * TS
NY, NX, NC = 4, 2, 2
NZ, NH = 4, 2
HALF = SB // 2
STEP = 1024
KT = TILE // STEP
MIB = 1 << 20
LANES = 128


def blk_moves(dy, dx, dc):
    spots = [(y, x, c) for y in range(NY) for x in range(NX) for c in range(NC)]
    index = lambda y, x, c: (y * NX + x) * NC + c
    return [(index(y, x, c), index(y ^ dy, x ^ dx, c ^ dc)) for y, x, c in spots]


def row_moves(dz, dx):
    spots = [(z, x) for z in range(NZ) for x in range(NH)]
    return [(z * NH + x, (z ^ dz) * NH + (x ^ dx)) for z, x in spots]


def move(value, dy=0, dx=0, dc=0):
    return lax.ppermute(value, "blk", blk_moves(dy, dx, dc))


def move_row(value, dz=0, dx=0):
    return lax.ppermute(value, "row", row_moves(dz, dx))


def together(*values):
    return lax.optimization_barrier(values)


def live_slot(live, n):
    if n == 0:
        return jnp.where(live[0] == 1, 0, jnp.where(live[1] == 1, 1, 2))
    return jnp.where(live[3] == 1, 3, jnp.where(live[2] == 1, 2, 1))


def pick_kernel(live, columns, out, sems):
    copies = []
    for n in range(2):
        start = pl.multiple_of(live_slot(live, n) * TILE, TILE)
        for h in range(2):
            source = columns.at[pl.ds(h * HALF, HALF), pl.ds(start, TILE)]
            copies.append(pltpu.make_async_copy(source, out.at[2 * h + n], sems.at[n, h]))
    for copy in copies:
        copy.start()
    for copy in copies:
        copy.wait()


def pick_live(live_pairs, columns):
    return pl.pallas_call(
        pick_kernel,
        out_shape=jax.ShapeDtypeStruct((4, HALF, TILE), columns.dtype),
        in_specs=[pl.BlockSpec(memory_space=pltpu.SMEM), pl.BlockSpec(memory_space=pltpu.HBM)],
        out_specs=pl.BlockSpec(memory_space=pltpu.VMEM),
        scratch_shapes=[pltpu.SemaphoreType.DMA((2, 2))],
        compiler_params=pltpu.CompilerParams(vmem_limit_bytes=4 * MIB),
        name="pick_live",
    )(live_pairs, columns)


def load_kernel(live, amps, after, out, token, sems):
    token[...] = jnp.zeros_like(token)
    copies = []
    for n in range(2):
        for k in range(KT):
            start = pl.multiple_of(live_slot(live, n) * TILE + k * STEP, STEP)
            at = n * KT + k
            copies.append(pltpu.make_async_copy(amps.at[:, pl.ds(start, STEP)], out.at[at], sems.at[at]))
    for copy in copies:
        copy.start()
    for copy in copies:
        copy.wait()


def load_live(live_pairs, amplitudes, after):
    rows = amplitudes.shape[0]
    return pl.pallas_call(
        load_kernel,
        out_shape=(
            jax.ShapeDtypeStruct((2 * KT, rows, STEP), amplitudes.dtype),
            jax.ShapeDtypeStruct((8, 128), jnp.float32),
        ),
        in_specs=[pl.BlockSpec(memory_space=pltpu.SMEM)] + [pl.BlockSpec(memory_space=pl.ANY)] * 2,
        out_specs=(pl.BlockSpec(memory_space=pltpu.VMEM),) * 2,
        scratch_shapes=[pltpu.SemaphoreType.DMA((2 * KT,))],
        compiler_params=pltpu.CompilerParams(vmem_limit_bytes=40 * MIB),
        name="load_live",
    )(live_pairs, amplitudes, after)


def ladder_kernel(places, e, count, amps, cycle, before, *refs):
    pieces, outs, (token, total) = refs[:count], refs[count:-2], refs[-2:]
    token[...] = jnp.zeros_like(token)
    for n in range(2):
        held = {}
        for piece, index, slot, *place in places:
            if slot == n:
                held[tuple(place)] = pieces[piece].at[index] if index else pieces[piece]
        for k in range(KT):
            cols = slice(k * STEP, (k + 1) * STEP)
            block = jnp.concatenate(
                [held[dy, g, h][:, cols] for dy in range(NY) for g in range(NC) for h in range(2)]
            )
            term = lax.dot_general(
                block, amps[n * KT + k], (((1,), (1,)), ((), ())), preferred_element_type=jnp.float32
            )
            if n == k == 0:
                total[...] = term
            else:
                total[...] += term

    spot = lax.axis_index("blk")
    y, x, c = spot // (NX * NC), (spot // NC) % NX, spot % NC
    z = lax.axis_index("row") // NH
    for dz in range(NZ):
        dy = (z ^ dz) ^ y
        for core in range(NC):
            here = (dy * NC + (c ^ core)) * SB
            there = (((z ^ dz) * NX + (x ^ e)) * NC + core) * SB
            there = pl.ds(pl.multiple_of(there, SB), SB)
            rows = slice(core * SB, (core + 1) * SB)
            value = total[pl.ds(pl.multiple_of(here, SB), SB), :] + jnp.concatenate(
                [cycle[n, there, :] for n in range(cycle.shape[0])], axis=1
            )
            if dz == 2 and len(outs) > NZ:
                mine = x == lax.axis_index("row") % NH
                outs[2][rows, :] = jnp.where(mine, before[rows, :], value)
                outs[NZ][rows, :] = jnp.where(mine, value, before[rows, :])
            else:
                outs[dz][rows, :] = value


def ladder(e, amplitudes, cycle, before, pieces, exchange=False):
    places = [(n, *place) for n, (_, held) in enumerate(pieces) for place in held]
    rows, q = amplitudes.shape[1], NY * NC * SB
    out = jax.ShapeDtypeStruct((q // NZ, rows), jnp.float32)
    return pl.pallas_call(
        functools.partial(ladder_kernel, places, e, len(pieces)),
        out_shape=(out,) * (NZ + exchange) + (jax.ShapeDtypeStruct((8, 128), jnp.float32),),
        in_specs=[pl.BlockSpec(memory_space=pltpu.VMEM)] * (3 + len(pieces)),
        out_specs=[pl.BlockSpec(memory_space=pltpu.VMEM)] * (NZ + exchange + 1),
        scratch_shapes=[pltpu.VMEM((q, rows), jnp.float32)],
        compiler_params=pltpu.CompilerParams(vmem_limit_bytes=24 * MIB),
        cost_estimate=pl.CostEstimate(
            flops=2 * q * rows * 2 * TILE, bytes_accessed=2 * q * 2 * TILE, transcendentals=0
        ),
        name="ladder",
    )(amplitudes, cycle, before, *[array for array, _ in pieces])


def pack_kernel(*refs):
    *blocks, out = refs
    for e, block in enumerate(blocks):
        for n in range(block.shape[0] // HALF):
            at = (e * (block.shape[0] // HALF) + n) * block.shape[1]
            out[0, :, at : at + block.shape[1]] = block[n * HALF : (n + 1) * HALF, :]


def pack(*blocks):
    return pl.pallas_call(
        pack_kernel,
        out_shape=jax.ShapeDtypeStruct((1, HALF, TILE), blocks[0].dtype),
        in_specs=[pl.BlockSpec(memory_space=pltpu.VMEM)] * len(blocks),
        out_specs=pl.BlockSpec(memory_space=pltpu.VMEM),
        compiler_params=pltpu.CompilerParams(vmem_limit_bytes=4 * MIB),
        name="pack",
    )(*blocks)


def cycle_kernel(places, width, slab_amps, token, *refs):
    blocks, out, turned, rows_of = refs[:-3], refs[-3], refs[-2], refs[-1]
    k_local, i_local, ac = slab_amps.shape
    a_all, per = ac // SB, rows_of.shape[-1] // SB
    for part in range(k_local // per):
        held = [slab_amps[part * per + n].astype(jnp.float32) for n in range(per)]
        for a in range(a_all):
            row = jnp.concatenate([k[:, a * SB : (a + 1) * SB] for k in held], axis=1)
            rows_of[part, pl.ds(a, i_local, stride=a_all), :] = row
    slab = jnp.concatenate([rows_of[part] for part in range(k_local // per)], axis=1).astype(jnp.bfloat16)
    spot = lax.axis_index("blk")
    y, x, c = spot // (NX * NC), (spot // NC) % NX, spot % NC
    pairs, depth = slab.shape
    for piece, index, half, dy, e, g in places:
        tiles = []
        for n in range(depth // HALF):
            at = (half * (depth // HALF) + n) * width
            tiles.append(blocks[piece][(*index, slice(None), slice(at, at + width))])
        term = jnp.dot(slab, jnp.concatenate(tiles), preferred_element_type=jnp.float32)
        block = ((y ^ dy) * NX + (x ^ e)) * NC + (c ^ g)
        turned[pl.ds(pl.multiple_of(block * width, width), width), :] = term.T
    for b in range(SB):
        rows = turned[pl.ds(b, OW, stride=SB), :].T
        for i in range(0, pairs // a_all, 2):
            both = [rows[at * a_all : (at + 1) * a_all] for at in (i, i + 1)]
            out[i // 2, pl.ds(b, a_all, stride=SB), :] = jnp.concatenate(both, axis=1)


def cycle_sums(slab_amplitudes, pieces, token):
    k_local, i_local, ac = slab_amplitudes.shape
    a_all, depth = ac // SB, k_local * SB
    arrays = list({id(array): array for array, *_ in pieces}.values())
    order = [id(array) for array in arrays]
    places = [(order.index(id(array)), index, half, dy, e, g) for array, index, half, dy, e, g in pieces]
    width = OW * SB // (NY * NX * NC)
    return pl.pallas_call(
        functools.partial(cycle_kernel, places, width),
        out_shape=jax.ShapeDtypeStruct((i_local // 2, a_all * SB, 2 * OW), jnp.float32),
        in_specs=[pl.BlockSpec(memory_space=pltpu.VMEM)] * (2 + len(arrays)),
        out_specs=pl.BlockSpec(memory_space=pltpu.VMEM),
        scratch_shapes=[
            pltpu.VMEM((OW * SB, i_local * a_all), jnp.float32),
            pltpu.VMEM((depth // LANES, i_local * a_all, LANES), jnp.float32),
        ],
        compiler_params=pltpu.CompilerParams(vmem_limit_bytes=16 * MIB),
        cost_estimate=pl.CostEstimate(
            flops=2 * i_local * a_all * depth * OW * SB, bytes_accessed=8 * MIB, transcendentals=0
        ),
        name="cycle",
    )(slab_amplitudes, token, *arrays)


def sum_beside(parts):
    return parts[0] + move_row(parts[1], dz=1) + move_row(parts[3], dz=3)


def per_device(amplitudes, integrals, live_pairs, slab_amplitudes, cycle_integrals):
    def swap(*arrays):
        return (jnp.concatenate(arrays), move(jnp.concatenate(arrays), dc=1))

    own = pick_live(live_pairs, integrals.T)
    below, above, beside = move(own, dy=1), move(own, dy=3), move(own, dx=1)
    cycle_beside, cycle_far = move(cycle_integrals, dx=1), move(cycle_integrals, dy=2)
    live_amps, token = load_live(live_pairs, amplitudes, own)
    cycle_beside, token = together(cycle_beside, token)
    pair = pack(cycle_integrals, cycle_beside)
    below, above, beside, cycle_far, pair, token = together(below, above, beside, cycle_far, pair, token)

    far = pack(cycle_far)
    from_above = move(jnp.concatenate([below[0:2], beside[0:2], pair]), dy=3)
    from_below = move(jnp.concatenate([above[2:4], beside[0:2], pair]), dy=1)
    across = move(jnp.concatenate([below[2:4], above[2:4], far]), dx=1)
    hop = swap(own, below, above, beside, pair, far)

    from_above, from_below, across = together(from_above, from_below, across)
    last_above = move(jnp.concatenate([from_below[2:3], across[0:1]]), dy=3)
    last_below = move(jnp.concatenate([from_above[3:4], across[3:4]]), dy=1)
    hop_near = swap(from_above[0:2], from_below[0:2], from_above[4:5], from_below[4:5], across[4:5])
    hop_far = swap(from_above[2:4], from_below[2:4], across[0:4])

    blocks = []
    for g in range(NC):
        for e in range(2):
            blocks += [(hop[g], (16,), e, 0, e, g), (hop_near[g], (4,), e, 3, e, g), (hop_near[g], (5,), e, 1, e, g)]
        blocks += [(hop[g], (17,), 0, 2, 0, g), (hop_near[g], (6,), 0, 2, 1, g)]
    cycle = cycle_sums(slab_amplitudes, blocks, token)
    token, hop_1 = together(token, hop_far[1])
    hop_far = (hop_far[0], hop_1)

    halves = [(h, n) for h in range(2) for n in range(2)]
    near = []
    for g in range(NC):
        places = [((4 * at + 2 * h + n,), n, dy, g, h) for at, dy in enumerate((0, 1, 3)) for h, n in halves]
        near += [(hop[g], places), (hop_near[g], [((2 * h + n,), n, 2, g, h) for h, n in halves])]
    *near, token = ladder(0, live_amps, cycle, token, near)
    near_sum = sum_beside(near)

    last_above, last_below, before = together(last_above, last_below, near[2])
    far = []
    for g in range(NC):
        places = [((2 * at + n,), n, dy, g, 0) for at, dy in enumerate((3, 1)) for n in range(2)]
        places += [((4 + 2 * at + n,), n, dy, g, 1) for at, dy in enumerate((1, 3)) for n in range(2)]
        far += [(hop[g], [((12 + 2 * h + n,), n, 0, g, h) for h, n in halves]), (hop_far[g], places)]
    for g, both in enumerate(swap(last_above, last_below)):
        far.append((both, [((2 * n + h,), n, 2, g, h) for h, n in halves]))
    *far, other, _ = ladder(1, live_amps, cycle, before, far, exchange=True)
    far_sum = sum_beside(far)

    mine = lax.axis_index("row") % NH == (lax.axis_index("blk") // NC) % NX
    total = jnp.where(mine, near_sum, far_sum) + move_row(jnp.where(mine, far_sum, near_sum), dx=1)
    total = total + move_row(far[2], dz=2) + move_row(other, dz=2, dx=1)
    return total.astype(jnp.bfloat16).T


def solution(mesh):
    return jax.shard_map(
        per_device,
        mesh=mesh,
        in_specs=(
            P("blk", "row"),
            P("row", "blk"),
            P("row"),
            P("row", "blk", None),
            P("row", "blk"),
        ),
        out_specs=P("blk", "row"),
        check_vma=False,
    )
```

```python
import functools

import jax
import jax.numpy as jnp
from jax import lax
from jax.experimental import pallas as pl
from jax.experimental.pallas import tpu as pltpu
from jax.sharding import PartitionSpec as P

OW = 64
TS = 64
SB = 32
TILE = TS * TS
NY, NX, NC = 4, 2, 2
NZ, NH = 4, 2
HALF = SB // 2
STEP = 1024
KT = TILE // STEP
MIB = 1 << 20
LANES = 128


def blk_moves(dy, dx, dc):
    spots = [(y, x, c) for y in range(NY) for x in range(NX) for c in range(NC)]
    index = lambda y, x, c: (y * NX + x) * NC + c
    return [(index(y, x, c), index(y ^ dy, x ^ dx, c ^ dc)) for y, x, c in spots]


def row_moves(dz, dx):
    spots = [(z, x) for z in range(NZ) for x in range(NH)]
    return [(z * NH + x, (z ^ dz) * NH + (x ^ dx)) for z, x in spots]


def move(value, dy=0, dx=0, dc=0):
    return lax.ppermute(value, "blk", blk_moves(dy, dx, dc))


def move_row(value, dz=0, dx=0):
    return lax.ppermute(value, "row", row_moves(dz, dx))


def together(*values):
    return lax.optimization_barrier(values)


def live_slot(live, n):
    if n == 0:
        return jnp.where(live[0] == 1, 0, jnp.where(live[1] == 1, 1, 2))
    return jnp.where(live[3] == 1, 3, jnp.where(live[2] == 1, 2, 1))


def pick_kernel(live, columns, out, sems):
    copies = []
    for n in range(2):
        start = pl.multiple_of(live_slot(live, n) * TILE, TILE)
        for h in range(2):
            source = columns.at[pl.ds(h * HALF, HALF), pl.ds(start, TILE)]
            copies.append(pltpu.make_async_copy(source, out.at[2 * h + n], sems.at[n, h]))
    for copy in copies:
        copy.start()
    for copy in copies:
        copy.wait()


def pick_live(live_pairs, columns):
    return pl.pallas_call(
        pick_kernel,
        out_shape=jax.ShapeDtypeStruct((4, HALF, TILE), columns.dtype),
        in_specs=[pl.BlockSpec(memory_space=pltpu.SMEM), pl.BlockSpec(memory_space=pltpu.HBM)],
        out_specs=pl.BlockSpec(memory_space=pltpu.VMEM),
        scratch_shapes=[pltpu.SemaphoreType.DMA((2, 2))],
        compiler_params=pltpu.CompilerParams(vmem_limit_bytes=4 * MIB),
        name="pick_live",
    )(live_pairs, columns)


def load_kernel(live, amps, after, out, token, sems):
    token[...] = jnp.zeros_like(token)
    copies = []
    for n in range(2):
        for k in range(KT):
            start = pl.multiple_of(live_slot(live, n) * TILE + k * STEP, STEP)
            at = n * KT + k
            copies.append(pltpu.make_async_copy(amps.at[:, pl.ds(start, STEP)], out.at[at], sems.at[at]))
    for copy in copies:
        copy.start()
    for copy in copies:
        copy.wait()


def load_live(live_pairs, amplitudes, after):
    rows = amplitudes.shape[0]
    return pl.pallas_call(
        load_kernel,
        out_shape=(
            jax.ShapeDtypeStruct((2 * KT, rows, STEP), amplitudes.dtype),
            jax.ShapeDtypeStruct((8, 128), jnp.float32),
        ),
        in_specs=[pl.BlockSpec(memory_space=pltpu.SMEM)] + [pl.BlockSpec(memory_space=pl.ANY)] * 2,
        out_specs=(pl.BlockSpec(memory_space=pltpu.VMEM),) * 2,
        scratch_shapes=[pltpu.SemaphoreType.DMA((2 * KT,))],
        compiler_params=pltpu.CompilerParams(vmem_limit_bytes=40 * MIB),
        name="load_live",
    )(live_pairs, amplitudes, after)


def ladder_kernel(places, e, count, amps, cycle, before, *refs):
    pieces, outs, (token, total) = refs[:count], refs[count:-2], refs[-2:]
    token[...] = jnp.zeros_like(token)
    for n in range(2):
        held = {}
        for piece, index, slot, *place in places:
            if slot == n:
                held[tuple(place)] = pieces[piece].at[index] if index else pieces[piece]
        for k in range(KT):
            cols = slice(k * STEP, (k + 1) * STEP)
            block = jnp.concatenate(
                [held[dy, g, h][:, cols] for dy in range(NY) for g in range(NC) for h in range(2)]
            )
            term = lax.dot_general(
                block, amps[n * KT + k], (((1,), (1,)), ((), ())), preferred_element_type=jnp.float32
            )
            if n == k == 0:
                total[...] = term
            else:
                total[...] += term

    spot = lax.axis_index("blk")
    y, x, c = spot // (NX * NC), (spot // NC) % NX, spot % NC
    z = lax.axis_index("row") // NH
    for dz in range(NZ):
        dy = (z ^ dz) ^ y
        for core in range(NC):
            here = (dy * NC + (c ^ core)) * SB
            there = (((z ^ dz) * NX + (x ^ e)) * NC + core) * SB
            there = pl.ds(pl.multiple_of(there, SB), SB)
            rows = slice(core * SB, (core + 1) * SB)
            value = total[pl.ds(pl.multiple_of(here, SB), SB), :] + jnp.concatenate(
                [cycle[n, there, :] for n in range(cycle.shape[0])], axis=1
            )
            if dz == 2 and len(outs) > NZ:
                mine = x == lax.axis_index("row") % NH
                outs[2][rows, :] = jnp.where(mine, before[rows, :], value)
                outs[NZ][rows, :] = jnp.where(mine, value, before[rows, :])
            else:
                outs[dz][rows, :] = value


def ladder(e, amplitudes, cycle, before, pieces, exchange=False):
    places = [(n, *place) for n, (_, held) in enumerate(pieces) for place in held]
    rows, q = amplitudes.shape[1], NY * NC * SB
    out = jax.ShapeDtypeStruct((q // NZ, rows), jnp.float32)
    return pl.pallas_call(
        functools.partial(ladder_kernel, places, e, len(pieces)),
        out_shape=(out,) * (NZ + exchange) + (jax.ShapeDtypeStruct((8, 128), jnp.float32),),
        in_specs=[pl.BlockSpec(memory_space=pltpu.VMEM)] * (3 + len(pieces)),
        out_specs=[pl.BlockSpec(memory_space=pltpu.VMEM)] * (NZ + exchange + 1),
        scratch_shapes=[pltpu.VMEM((q, rows), jnp.float32)],
        compiler_params=pltpu.CompilerParams(vmem_limit_bytes=24 * MIB),
        cost_estimate=pl.CostEstimate(
            flops=2 * q * rows * 2 * TILE, bytes_accessed=2 * q * 2 * TILE, transcendentals=0
        ),
        name="ladder",
    )(amplitudes, cycle, before, *[array for array, _ in pieces])


def pack_kernel(*refs):
    *blocks, out = refs
    for e, block in enumerate(blocks):
        for n in range(block.shape[0] // HALF):
            at = (e * (block.shape[0] // HALF) + n) * block.shape[1]
            out[0, :, at : at + block.shape[1]] = block[n * HALF : (n + 1) * HALF, :]


def pack(*blocks):
    return pl.pallas_call(
        pack_kernel,
        out_shape=jax.ShapeDtypeStruct((1, HALF, TILE), blocks[0].dtype),
        in_specs=[pl.BlockSpec(memory_space=pltpu.VMEM)] * len(blocks),
        out_specs=pl.BlockSpec(memory_space=pltpu.VMEM),
        compiler_params=pltpu.CompilerParams(vmem_limit_bytes=4 * MIB),
        name="pack",
    )(*blocks)


def cycle_kernel(places, width, slab_amps, token, *refs):
    blocks, out, turned, rows_of = refs[:-3], refs[-3], refs[-2], refs[-1]
    k_local, i_local, ac = slab_amps.shape
    a_all, per = ac // SB, rows_of.shape[-1] // SB
    for part in range(k_local // per):
        held = [slab_amps[part * per + n].astype(jnp.float32) for n in range(per)]
        for a in range(a_all):
            row = jnp.concatenate([k[:, a * SB : (a + 1) * SB] for k in held], axis=1)
            rows_of[part, pl.ds(a, i_local, stride=a_all), :] = row
    slab = jnp.concatenate([rows_of[part] for part in range(k_local // per)], axis=1).astype(jnp.bfloat16)
    spot = lax.axis_index("blk")
    y, x, c = spot // (NX * NC), (spot // NC) % NX, spot % NC
    pairs, depth = slab.shape
    for piece, index, half, dy, e, g in places:
        tiles = []
        for n in range(depth // HALF):
            at = (half * (depth // HALF) + n) * width
            tiles.append(blocks[piece][(*index, slice(None), slice(at, at + width))])
        term = jnp.dot(slab, jnp.concatenate(tiles), preferred_element_type=jnp.float32)
        block = ((y ^ dy) * NX + (x ^ e)) * NC + (c ^ g)
        turned[pl.ds(pl.multiple_of(block * width, width), width), :] = term.T
    for b in range(SB):
        rows = turned[pl.ds(b, OW, stride=SB), :].T
        for i in range(0, pairs // a_all, 2):
            both = [rows[at * a_all : (at + 1) * a_all] for at in (i, i + 1)]
            out[i // 2, pl.ds(b, a_all, stride=SB), :] = jnp.concatenate(both, axis=1)


def cycle_sums(slab_amplitudes, pieces, token):
    k_local, i_local, ac = slab_amplitudes.shape
    a_all, depth = ac // SB, k_local * SB
    arrays = list({id(array): array for array, *_ in pieces}.values())
    order = [id(array) for array in arrays]
    places = [(order.index(id(array)), index, half, dy, e, g) for array, index, half, dy, e, g in pieces]
    width = OW * SB // (NY * NX * NC)
    return pl.pallas_call(
        functools.partial(cycle_kernel, places, width),
        out_shape=jax.ShapeDtypeStruct((i_local // 2, a_all * SB, 2 * OW), jnp.float32),
        in_specs=[pl.BlockSpec(memory_space=pltpu.VMEM)] * (2 + len(arrays)),
        out_specs=pl.BlockSpec(memory_space=pltpu.VMEM),
        scratch_shapes=[
            pltpu.VMEM((OW * SB, i_local * a_all), jnp.float32),
            pltpu.VMEM((depth // LANES, i_local * a_all, LANES), jnp.float32),
        ],
        compiler_params=pltpu.CompilerParams(vmem_limit_bytes=16 * MIB),
        cost_estimate=pl.CostEstimate(
            flops=2 * i_local * a_all * depth * OW * SB, bytes_accessed=8 * MIB, transcendentals=0
        ),
        name="cycle",
    )(slab_amplitudes, token, *arrays)


def sum_beside(parts):
    return parts[0] + move_row(parts[1], dz=1) + move_row(parts[3], dz=3)


def per_device(amplitudes, integrals, live_pairs, slab_amplitudes, cycle_integrals):
    def swap(*arrays):
        return (jnp.concatenate(arrays), move(jnp.concatenate(arrays), dc=1))

    own = pick_live(live_pairs, integrals.T)
    below, above, beside = move(own, dy=1), move(own, dy=3), move(own, dx=1)
    cycle_beside, cycle_far = move(cycle_integrals, dx=1), move(cycle_integrals, dy=2)
    live_amps, token = load_live(live_pairs, amplitudes, own)
    cycle_beside, token = together(cycle_beside, token)
    pair = pack(cycle_integrals, cycle_beside)
    below, above, beside, pair, token = together(below, above, beside, pair, token)

    far = pack(cycle_far)
    from_above = move(jnp.concatenate([below[0:2], beside[0:2], pair]), dy=3)
    from_below = move(jnp.concatenate([above[2:4], beside[0:2], pair]), dy=1)
    across = move(jnp.concatenate([below[2:4], above[2:4], far]), dx=1)
    hop = swap(own, below, above, beside, pair, far)

    from_above, from_below, across = together(from_above, from_below, across)
    last_above = move(jnp.concatenate([from_below[2:3], across[0:1]]), dy=3)
    last_below = move(jnp.concatenate([from_above[3:4], across[3:4]]), dy=1)
    hop_near = swap(from_above[0:2], from_below[0:2], from_above[4:5], from_below[4:5], across[4:5])
    hop_far = swap(from_above[2:4], from_below[2:4], across[0:4])

    blocks = []
    for g in range(NC):
        for e in range(2):
            blocks += [(hop[g], (16,), e, 0, e, g), (hop_near[g], (4,), e, 3, e, g), (hop_near[g], (5,), e, 1, e, g)]
        blocks += [(hop[g], (17,), 0, 2, 0, g), (hop_near[g], (6,), 0, 2, 1, g)]
    cycle = cycle_sums(slab_amplitudes, blocks, token)
    token, hop_1 = together(token, hop_far[1])
    hop_far = (hop_far[0], hop_1)

    halves = [(h, n) for h in range(2) for n in range(2)]
    near = []
    for g in range(NC):
        places = [((4 * at + 2 * h + n,), n, dy, g, h) for at, dy in enumerate((0, 1, 3)) for h, n in halves]
        near += [(hop[g], places), (hop_near[g], [((2 * h + n,), n, 2, g, h) for h, n in halves])]
    *near, token = ladder(0, live_amps, cycle, token, near)
    near_sum = sum_beside(near)

    last_above, last_below, before = together(last_above, last_below, near[2])
    far = []
    for g in range(NC):
        places = [((2 * at + n,), n, dy, g, 0) for at, dy in enumerate((3, 1)) for n in range(2)]
        places += [((4 + 2 * at + n,), n, dy, g, 1) for at, dy in enumerate((1, 3)) for n in range(2)]
        far += [(hop[g], [((12 + 2 * h + n,), n, 0, g, h) for h, n in halves]), (hop_far[g], places)]
    for g, both in enumerate(swap(last_above, last_below)):
        far.append((both, [((2 * n + h,), n, 2, g, h) for h, n in halves]))
    *far, other, _ = ladder(1, live_amps, cycle, before, far, exchange=True)
    far_sum = sum_beside(far)

    mine = lax.axis_index("row") % NH == (lax.axis_index("blk") // NC) % NX
    total = jnp.where(mine, near_sum, far_sum) + move_row(jnp.where(mine, far_sum, near_sum), dx=1)
    total = total + move_row(far[2], dz=2) + move_row(other, dz=2, dx=1)
    return total.astype(jnp.bfloat16).T


def solution(mesh):
    return jax.shard_map(
        per_device,
        mesh=mesh,
        in_specs=(
            P("blk", "row"),
            P("row", "blk"),
            P("row"),
            P("row", "blk", None),
            P("row", "blk"),
        ),
        out_specs=P("blk", "row"),
        check_vma=False,
    )
```
